512 devices in a mesh: feat: 32 (over z, x), rep: 16 (over y, core).
Axes of the slice: x: 4, y: 8, z: 8, core: 2. Of those that a mesh axis runs over, the one named last changes fastest.
Arguments:
- feature_table: bfloat16 [128, 16384], P('feat'), may hold values from -6 to 6
- node_ids: int32 [16, 6144], P('rep'), may hold values from 0 to 16383
- block_ids: int32 [16, 32, 4], P('rep'), may hold values from 0 to 47, as said below
- block_counts: int32 [16, 32], P('rep'), may hold values from 1 to 4, as said below
- adjacency: bfloat16 [16, 32, 4, 128, 128], P('rep'), may hold values from -0.25 to 0.25
- self_weight: bfloat16 [128, 256], replicated, may hold values from -0.375 to 0.375
- neigh_weight: bfloat16 [128, 256], replicated, may hold values from -0.375 to 0.375
- bias_vector: float32 [256], replicated, may hold values from -4 to 4
- cotangent: bfloat16 [16, 4096, 256], P('rep', 'feat'), may hold values from -6 to 6
Outputs:
- hidden: bfloat16 [16, 4096, 256], P('rep', 'feat')
- feature_grad: bfloat16 [16, 128, 6144], P('rep', 'feat')
- self_weight_grad: float32 [128, 256], replicated
- neigh_weight_grad: float32 [128, 256], replicated
- bias_grad: float32 [256], replicated
The draws below stay inside these ranges and needn't reach their ends.
Inputs may be any that keep to these rules, and one draw needn't show every extreme that they name: `block_ids`: the 4 entries of a destination block's list are distinct source blocks, including unused slots. `block_counts`: in every replica some destination block uses all 4 slots.
All inputs are finite; a program needn't handle non-finite values.
Results may differ from the reference program's by a relative error of at most 0.0075.
Values may be sent and summed in bfloat16 or wider, within the bound.
No kernel may reach another device: no remote copies, remote signals or barrier semaphores. Data moves between devices by JAX's collectives and lax.ppermute only.
A program may use at most 64 MiB of HBM per device.

```python
import jax
import jax.numpy as jnp
from jax import lax

F = 128
H = 256
BLK = 128
MAXB = 4
TABLE = 16384
DB = 32
SB = 48
DST = 4096
NODES = 6144
N_REP = 16


def draw_block_counts(key, part):
    key = jax.random.fold_in(key, 11)
    first_key, second_key = jax.random.split(key)
    counts = jax.random.randint(first_key, (N_REP, DB), 1, MAXB + 1)
    chosen = jax.random.randint(second_key, (N_REP, 1), 0, DB)
    places = lax.broadcasted_iota(jnp.int32, (N_REP, DB), 1)
    return jnp.where(places == chosen, MAXB, counts).astype(jnp.int32)


def draw_block_ids(key, part):
    key = jax.random.fold_in(key, 23)
    scores = jax.random.randint(key, (N_REP, DB, SB), 0, 1048576)
    scores = scores * SB + lax.broadcasted_iota(jnp.int32, (N_REP, DB, SB), 2)
    ordered = jnp.argsort(scores, axis=-1, stable=True)
    return ordered[:, :, :MAXB].astype(jnp.int32)


def set_ends(drawn, stream_key, least, largest):
    longest = drawn.shape.index(max(drawn.shape))
    spots = []
    for shift in (0, 1):
        where = [jax.random.randint(jax.random.fold_in(stream_key, axis), (), 0, length) for axis, length in enumerate(drawn.shape)]
        where[longest] = (where[longest] + shift) % drawn.shape[longest]
        spots.append(tuple(where))
    return drawn.at[spots[0]].set(least).at[spots[1]].set(largest)


def block_scale(stream_key, extent, pieces, smallest, high):
    level = 1.0
    for axis_at, parts in pieces:
        heights = jax.random.uniform(jax.random.fold_in(jax.random.fold_in(stream_key, 6), axis_at), (parts,), jnp.float32, smallest / len(pieces), high / len(pieces))
        level = level * jnp.repeat(jnp.exp(heights), extent[axis_at] // parts).reshape((-1,) + (1,) * (len(extent) - 1 - axis_at))
    return level


def centred(own_key, shape, scale, reach, shards=(), kind=jnp.bfloat16):
    gain = block_scale(own_key, shape, shards, -0.22, 0.18) if shards else 1.0
    array = jax.random.normal(own_key, shape, jnp.float32) * scale * gain
    return jnp.minimum(jnp.maximum(array, -reach), reach).astype(kind)


def setup_inputs(seed: int = 0) -> dict:
    key_list = jax.random.split(jax.random.key(seed), 10)
    return {
        "feature_table": centred(key_list[0], (F, TABLE), 1.0, 6.0, ((0, 32),)),
        "node_ids": set_ends(jax.random.randint(key_list[1], (N_REP, NODES), 0, TABLE), jax.random.fold_in(key_list[1], 1), 0, TABLE - 1).astype(jnp.int32),
        "block_ids": draw_block_ids(jax.random.fold_in(key_list[9], 71), 0),
        "block_counts": draw_block_counts(jax.random.fold_in(key_list[9], 71), 0),
        "adjacency": centred(key_list[4], (N_REP, DB, MAXB, BLK, BLK), (BLK * MAXB) ** -0.5, 0.25, ((0, 16),)),
        "self_weight": centred(key_list[5], (F, H), (2 * F) ** -0.5, 0.375),
        "neigh_weight": centred(key_list[6], (F, H), (2 * F) ** -0.5, 0.375),
        "bias_vector": centred(key_list[7], (H,), 1.0, 4.0, (), jnp.float32),
        "cotangent": centred(key_list[8], (N_REP, DST, H), 1.0, 6.0, ((0, 16), (1, 32))),
    }


def replica_step(feature_table, self_weight, neigh_weight, bias_vector, packed):
    node_ids, block_ids, block_counts, adjacency, cotangent = packed
    features = feature_table[:, node_ids]
    sources = features.reshape(F, SB, BLK)
    picked = sources[:, block_ids]
    alive_mask = lax.broadcasted_iota(jnp.int32, (DB, MAXB), 1) < block_counts[:, None]
    picked = jnp.where(alive_mask[None, :, :, None], picked, jnp.zeros_like(picked))
    adj_float = adjacency.astype(jnp.float32)
    summed = jnp.einsum('cbks,bksd->cbd', picked.astype(jnp.float32), adj_float)
    aggregate = summed.reshape(F, DST).astype(jnp.bfloat16)
    self_part = features[:, :DST]
    preact = jnp.dot(self_part.T, self_weight, preferred_element_type=jnp.float32)
    preact = preact + jnp.dot(aggregate.T, neigh_weight, preferred_element_type=jnp.float32) + bias_vector
    sigmoid_v = jax.nn.sigmoid(preact)
    hidden = (preact * sigmoid_v).astype(jnp.bfloat16)
    grad_pre = (cotangent.astype(jnp.float32) * sigmoid_v * (1.0 + preact * (1.0 - sigmoid_v))).astype(jnp.bfloat16)
    grad_self = jnp.dot(self_part, grad_pre, preferred_element_type=jnp.float32)
    grad_neigh = jnp.dot(aggregate, grad_pre, preferred_element_type=jnp.float32)
    grad_bias = jnp.sum(grad_pre.astype(jnp.float32), axis=0)
    agg_back = jnp.dot(neigh_weight, grad_pre.T, preferred_element_type=jnp.float32).astype(jnp.bfloat16)
    self_back = jnp.dot(self_weight, grad_pre.T, preferred_element_type=jnp.float32).astype(jnp.bfloat16)
    contrib = jnp.einsum('cbd,bksd->cbks', agg_back.reshape(F, DB, BLK).astype(jnp.float32), adj_float)
    onehot = ((block_ids[:, :, None] == jnp.arange(SB, dtype=jnp.int32)[None, None, :]) & alive_mask[:, :, None]).astype(jnp.float32)
    spread = jnp.einsum('cbks,bkn->cns', contrib, onehot, precision=lax.Precision.HIGHEST).reshape(F, NODES)
    padded_self = jnp.pad(self_back.astype(jnp.float32), ((0, 0), (0, NODES - DST)))
    feature_grad = (spread + padded_self).astype(jnp.bfloat16)
    return hidden, feature_grad, grad_self, grad_neigh, grad_bias


def reference(feature_table, node_ids, block_ids, block_counts, adjacency, self_weight, neigh_weight, bias_vector, cotangent):
    def stepper(packed):
        return replica_step(feature_table, self_weight, neigh_weight, bias_vector, packed)

    hidden, feature_grad, grad_self, grad_neigh, grad_bias = lax.map(stepper, (node_ids, block_ids, block_counts, adjacency, cotangent))
    factor = float(DST * N_REP) ** -0.5
    self_weight_grad = jnp.sum(grad_self, axis=0) * factor
    neigh_weight_grad = jnp.sum(grad_neigh, axis=0) * factor
    bias_grad = jnp.sum(grad_bias, axis=0) * factor
    return hidden, feature_grad, self_weight_grad, neigh_weight_grad, bias_grad
```

```python
import jax
import jax.numpy as jnp
from jax import lax
from jax.experimental import pallas as pl
from jax.experimental.pallas import tpu as pltpu
from jax.sharding import PartitionSpec as P

F32 = jnp.float32
BF16 = jnp.bfloat16
ADJ_PARTS = 8
LOW = 256
CHUNK = 512


def adj_copies(adj_hbm, adj_vmem, sems):
    per = adj_vmem.shape[0] // ADJ_PARTS
    return [
        pltpu.make_async_copy(
            adj_hbm.at[0, pl.ds(p * per, per)], adj_vmem.at[pl.ds(p * per, per)], sems.at[p]
        )
        for p in range(ADJ_PARTS)
    ]


def forward_kernel(
    ids_ref, counts_ref, nodes_ref, table_ref, adj_hbm, out_ref, adj, rows_f32, feats, staged, sems
):
    copies = adj_copies(adj_hbm, adj, sems)
    for copy in copies:
        copy.start()
    chans = table_ref.shape[0]
    groups = table_ref.shape[1] // LOW
    for q in range(groups):
        rows_f32[q * chans : (q + 1) * chans, :] = table_ref[:, q * LOW : (q + 1) * LOW].astype(F32)
    table_rows = rows_f32[...].astype(BF16)
    node_count = nodes_ref.shape[1]
    for start in range(0, node_count, CHUNK):
        ids = nodes_ref[:, start : start + CHUNK]
        low = ids & (LOW - 1)
        high = ids // LOW
        onehot = jnp.where(lax.broadcasted_iota(jnp.int32, (LOW, CHUNK), 0) == low, 1.0, 0.0)
        spread = jnp.dot(table_rows, onehot.astype(BF16), preferred_element_type=F32)
        group = lax.broadcasted_iota(jnp.int32, spread.shape, 0) // chans
        kept = jnp.where(group == high, spread, 0.0)
        two = jnp.sum(kept.reshape(-1, 8, CHUNK), axis=0)
        both = two + pltpu.roll(two, 4, 0)
        for j in range(CHUNK // 128):
            feats[start // 128 + j] = both[:, j * 128 : (j + 1) * 128]
    blocks, depth = ids_ref.shape[1], ids_ref.shape[2]
    side = adj.shape[3]
    upper = lax.broadcasted_iota(jnp.int32, (8, side), 0) < chans
    per = blocks // ADJ_PARTS
    for b in range(blocks):
        if b % per == 0:
            copies[b // per].wait()
        count = counts_ref[0, b]
        picked = [
            jnp.where(k < count, feats[ids_ref[0, b, k]], 0.0) for k in range(depth)
        ]
        lhs = jnp.concatenate(picked, axis=1).astype(BF16)
        agg = jnp.dot(lhs, adj[b].reshape(depth * side, side), preferred_element_type=F32)
        staged[b] = jnp.where(upper, feats[b], agg)
    out_ref[...] = staged[...].astype(BF16)


def dense_kernel(x_ref, sw_ref, nw_ref, bias_ref, cot_ref, hidden_ref, send_ref):
    feats = sw_ref.shape[0]
    hid = sw_ref.shape[1]
    sw = sw_ref[...].astype(F32).reshape(feats // 8, 8, hid)
    nw = nw_ref[...].astype(F32).reshape(feats // 8, 8, hid)
    upper = lax.broadcasted_iota(jnp.int32, sw.shape, 1) < 4
    even = jnp.where(upper, sw, pltpu.roll(nw, 4, 1))
    odd = jnp.where(upper, pltpu.roll(sw, 4, 1), nw)
    weight = jnp.concatenate([even, odd], axis=1).reshape(2 * feats, hid).astype(BF16)
    rows = x_ref.shape[2]
    x = x_ref[...].reshape(2 * feats, rows)
    preact = lax.dot_general(x, weight, (((0,), (0,)), ((), ())), preferred_element_type=F32)
    preact = preact + bias_ref[...]
    sig = jax.nn.sigmoid(preact)
    hidden_ref[0] = (preact * sig).astype(BF16)
    grad_pre = (cot_ref[0].astype(F32) * sig * (1.0 + preact * (1.0 - sig))).astype(BF16)
    grads = jnp.dot(x, grad_pre, preferred_element_type=F32)
    back = lax.dot_general(
        weight, grad_pre, (((1,), (1,)), ((), ())), preferred_element_type=F32
    )
    bias_sum = jnp.sum(grad_pre.astype(F32), axis=0, keepdims=True)
    peers = x_ref.shape[0]
    half = hid // 2
    tail = split_rows(bias_sum[:, :half], bias_sum[:, half:])
    send_ref[...] = jnp.concatenate(
        [
            back.reshape(peers, 8, rows),
            grads[:, :half].reshape(peers, 8, half),
            grads[:, half:].reshape(peers, 8, half),
            jnp.broadcast_to(tail[None], (peers, 8, half)),
        ],
        axis=1,
    ).astype(BF16)


def split_rows(first, second):
    place = lax.broadcasted_iota(jnp.int32, (8, first.shape[1]), 0)
    first_hi = first.astype(BF16).astype(F32)
    second_hi = second.astype(BF16).astype(F32)
    out = jnp.where(place == 0, first_hi, 0.0)
    out = jnp.where(place == 1, second_hi, out)
    out = jnp.where(place == 2, first - first_hi, out)
    return jnp.where(place == 3, second - second_hi, out)


def feat_sum_kernel(got_ref, out_ref):
    total = jnp.sum(got_ref[...].astype(F32)[:, 8:, :], axis=0)
    low = total[16:24]
    tail = split_rows(low[0:1] + low[2:3], low[1:2] + low[3:4])
    whole = jnp.concatenate([total[:16], tail, jnp.zeros_like(tail)], axis=0).astype(BF16)
    out_ref[...] = jnp.broadcast_to(whole[None], out_ref.shape)


def rep_sum_kernel(factor, got_ref, out_ref, bias_ref):
    total = jnp.sum(got_ref[...].astype(F32), axis=0)
    low = total[16:24]
    bias_ref[...] = factor * jnp.concatenate([low[0:1] + low[2:3], low[1:2] + low[3:4]], axis=1)
    out_ref[...] = jnp.broadcast_to((factor * total[:16]).astype(BF16)[None], out_ref.shape)


def assemble_kernel(got_ref, self_ref, neigh_ref):
    peers = got_ref.shape[0]
    side = got_ref.shape[2]
    got = got_ref[...].astype(F32).reshape(peers // 2, 32, side)
    for h in range(2):
        even = got[:, 8 * h : 8 * h + 8]
        odd = got[:, 16 + 8 * h : 24 + 8 * h]
        upper = lax.broadcasted_iota(jnp.int32, even.shape, 1) < 4
        first = jnp.where(upper, even, pltpu.roll(odd, 4, 1))
        second = jnp.where(upper, pltpu.roll(even, 4, 1), odd)
        self_ref[:, h * side : (h + 1) * side] = first.reshape(peers * 4, side)
        neigh_ref[:, h * side : (h + 1) * side] = second.reshape(peers * 4, side)


def backward_kernel(ids_ref, counts_ref, got_ref, adj_hbm, out_ref, adj, acc, sems):
    copies = adj_copies(adj_hbm, adj, sems)
    for copy in copies:
        copy.start()
    acc[...] = jnp.zeros_like(acc)
    blocks, depth = ids_ref.shape[1], ids_ref.shape[2]
    side = adj.shape[3]
    sources = acc.shape[0] - 1
    per = blocks // ADJ_PARTS
    for b in range(blocks):
        if b % per == 0:
            copies[b // per].wait()
        count = counts_ref[0, b]
        lhs = got_ref[b, 0:16, :]
        contrib = lax.dot_general(
            lhs,
            adj[b].reshape(depth * side, side),
            (((1,), (1,)), ((), ())),
            preferred_element_type=F32,
        )
        for k in range(depth):
            place = jnp.where(k < count, ids_ref[0, b, k], sources)
            acc[place] = acc[place] + contrib[0:8, k * side : (k + 1) * side]
    chans = out_ref.shape[1]
    for n in range(sources):
        total = pltpu.roll(acc[n], 4, 0)
        if n < blocks:
            total = total + got_ref[n, 0:16, :].astype(F32)[0:8]
        out_ref[0, :, n * side : (n + 1) * side] = total[0:chans].astype(BF16)


SMEM = pl.BlockSpec(memory_space=pltpu.SMEM)
VMEM = pl.BlockSpec(memory_space=pltpu.VMEM)
HBM = pl.BlockSpec(memory_space=pltpu.HBM)


def params(mib):
    return pltpu.CompilerParams(vmem_limit_bytes=mib * 1024 * 1024)


def local(
    feature_table,
    node_ids,
    block_ids,
    block_counts,
    adjacency,
    self_weight,
    neigh_weight,
    bias_vector,
    cotangent,
):
    chans = feature_table.shape[0]
    node_count = node_ids.shape[1]
    blocks, depth, side = adjacency.shape[1:4]
    sources = node_count // side
    peers = lax.axis_size("feat")
    reps = lax.axis_size("rep")
    feats, hid = self_weight.shape
    rows = cotangent.shape[1]
    sent = pl.pallas_call(
        forward_kernel,
        out_shape=jax.ShapeDtypeStruct((peers, 8, side), BF16),
        in_specs=[SMEM, SMEM, VMEM, VMEM, HBM],
        out_specs=VMEM,
        scratch_shapes=[
            pltpu.VMEM(adjacency.shape[1:], BF16),
            pltpu.VMEM((feature_table.shape[1] // LOW * chans, LOW), F32),
            pltpu.VMEM((sources, 8, side), F32),
            pltpu.VMEM((peers, 8, side), F32),
            pltpu.SemaphoreType.DMA((ADJ_PARTS,)),
        ],
        compiler_params=params(24),
        name="forward",
    )(block_ids, block_counts, node_ids, feature_table, adjacency)
    arrived = lax.all_to_all(sent, "feat", split_axis=0, concat_axis=0, tiled=True)
    hidden, back = pl.pallas_call(
        dense_kernel,
        out_shape=(
            jax.ShapeDtypeStruct(cotangent.shape, BF16),
            jax.ShapeDtypeStruct((peers, 32, side), BF16),
        ),
        in_specs=[VMEM] * 5,
        out_specs=(VMEM, VMEM),
        compiler_params=params(24),
        name="dense",
    )(arrived, self_weight, neigh_weight, bias_vector.reshape(1, hid), cotangent)
    got = lax.all_to_all(back, "feat", split_axis=0, concat_axis=0, tiled=True)
    copies = pl.pallas_call(
        feat_sum_kernel,
        out_shape=jax.ShapeDtypeStruct((reps, 32, side), BF16),
        in_specs=[VMEM],
        out_specs=VMEM,
        name="feat_sum",
    )(got)
    over_rep = lax.all_to_all(copies, "rep", split_axis=0, concat_axis=0, tiled=True)
    feature_grad = pl.pallas_call(
        backward_kernel,
        out_shape=jax.ShapeDtypeStruct((1, chans, node_count), BF16),
        in_specs=[SMEM, SMEM, VMEM, HBM],
        out_specs=VMEM,
        scratch_shapes=[
            pltpu.VMEM(adjacency.shape[1:], BF16),
            pltpu.VMEM((sources + 1, 8, side), F32),
            pltpu.SemaphoreType.DMA((ADJ_PARTS,)),
        ],
        compiler_params=params(24),
        cost_estimate=pl.CostEstimate(
            flops=2 * 16 * adjacency.size, bytes_accessed=2 * adjacency.size, transcendentals=0
        ),
        name="spread_back",
    )(block_ids, block_counts, got, adjacency)
    factor = float(rows * peers * reps) ** (-0.5)
    pieces, bias_grad = pl.pallas_call(
        lambda *refs: rep_sum_kernel(factor, *refs),
        out_shape=(
            jax.ShapeDtypeStruct((peers, 16, side), BF16),
            jax.ShapeDtypeStruct((1, hid), F32),
        ),
        in_specs=[VMEM],
        out_specs=(VMEM, VMEM),
        name="rep_sum",
    )(over_rep)
    whole = lax.all_to_all(pieces, "feat", split_axis=0, concat_axis=0, tiled=True)
    self_grad, neigh_grad = pl.pallas_call(
        assemble_kernel,
        out_shape=(
            jax.ShapeDtypeStruct((feats, hid), F32),
            jax.ShapeDtypeStruct((feats, hid), F32),
        ),
        in_specs=[VMEM],
        out_specs=(VMEM, VMEM),
        name="assemble",
    )(whole)
    return hidden, feature_grad, self_grad, neigh_grad, bias_grad.reshape(hid)


def solution(mesh):
    return jax.shard_map(
        local,
        mesh=mesh,
        in_specs=(
            P("feat", None),
            P("rep", None),
            P("rep", None, None),
            P("rep", None),
            P("rep", None, None, None, None),
            P(),
            P(),
            P(),
            P("rep", "feat", None),
        ),
        out_specs=(P("rep", "feat", None), P("rep", "feat", None), P(), P(), P()),
        check_vma=False,
    )
```

```python
import jax
import jax.numpy as jnp
from jax import lax
from jax.experimental import pallas as pl
from jax.experimental.pallas import tpu as pltpu
from jax.sharding import PartitionSpec as P

F32 = jnp.float32
BF16 = jnp.bfloat16
ADJ_PARTS = 8
LOW = 256
CHUNK = 512
FWD_MIB = 58


def forward_kernel(
    lists_hbm,
    counts_hbm,
    nodes_hbm,
    table_hbm,
    adj_hbm,
    out_ref,
    adj,
    ids_ref,
    counts_ref,
    nodes_ref,
    table_ref,
    rows_f32,
    feats,
    staged,
    sems,
):
    per = adj.shape[0] // ADJ_PARTS
    inputs = [
        pltpu.make_async_copy(table_hbm, table_ref, sems.at[ADJ_PARTS]),
        pltpu.make_async_copy(nodes_hbm, nodes_ref, sems.at[ADJ_PARTS + 1]),
    ]
    lists = [
        pltpu.make_async_copy(lists_hbm, ids_ref, sems.at[ADJ_PARTS + 2]),
        pltpu.make_async_copy(counts_hbm, counts_ref, sems.at[ADJ_PARTS + 3]),
    ]
    copies = [
        pltpu.make_async_copy(
            adj_hbm.at[0, pl.ds(p * per, per)], adj.at[pl.ds(p * per, per)], sems.at[p]
        )
        for p in range(ADJ_PARTS)
    ]
    for copy in inputs + lists + copies:
        copy.start()
    for copy in inputs:
        copy.wait()
    chans = table_ref.shape[0]
    groups = table_ref.shape[1] // LOW
    for q in range(groups):
        rows_f32[q * chans : (q + 1) * chans, :] = table_ref[:, q * LOW : (q + 1) * LOW].astype(F32)
    table_rows = rows_f32[...].astype(BF16)
    node_count = nodes_ref.shape[1]
    for start in range(0, node_count, CHUNK):
        ids = nodes_ref[:, start : start + CHUNK]
        low = ids & (LOW - 1)
        high = ids // LOW
        onehot = jnp.where(lax.broadcasted_iota(jnp.int32, (LOW, CHUNK), 0) == low, 1.0, 0.0)
        spread = jnp.dot(table_rows, onehot.astype(BF16), preferred_element_type=F32)
        group = lax.broadcasted_iota(jnp.int32, spread.shape, 0) // chans
        kept = jnp.where(group == high, spread, 0.0)
        two = jnp.sum(kept.reshape(-1, 8, CHUNK), axis=0)
        both = two + pltpu.roll(two, 4, 0)
        for j in range(CHUNK // 128):
            feats[start // 128 + j] = both[:, j * 128 : (j + 1) * 128]
    for copy in lists:
        copy.wait()
    depth, blocks = ids_ref.shape[1], ids_ref.shape[2]
    side = adj.shape[3]
    upper = lax.broadcasted_iota(jnp.int32, (8, side), 0) < chans
    for b in range(blocks):
        if b % per == 0:
            copies[b // per].wait()
        count = counts_ref[0, b]
        picked = [
            jnp.where(k < count, feats[ids_ref[0, k, b]], 0.0) for k in range(depth)
        ]
        lhs = jnp.concatenate(picked, axis=1).astype(BF16)
        agg = jnp.dot(lhs, adj[b].reshape(depth * side, side), preferred_element_type=F32)
        staged[b] = jnp.where(upper, feats[b], agg)
    out_ref[...] = staged[...].astype(BF16)


def dense_kernel(x_ref, sw_ref, nw_ref, bias_ref, cot_ref, hidden_ref, back_ref, send_ref):
    feats = sw_ref.shape[0]
    hid = sw_ref.shape[1]
    sw = sw_ref[...].astype(F32).reshape(feats // 8, 8, hid)
    nw = nw_ref[...].astype(F32).reshape(feats // 8, 8, hid)
    upper = lax.broadcasted_iota(jnp.int32, sw.shape, 1) < 4
    even = jnp.where(upper, sw, pltpu.roll(nw, 4, 1))
    odd = jnp.where(upper, pltpu.roll(sw, 4, 1), nw)
    weight = jnp.concatenate([even, odd], axis=1).reshape(2 * feats, hid).astype(BF16)
    rows = x_ref.shape[2]
    x = x_ref[...].reshape(2 * feats, rows)
    preact = lax.dot_general(x, weight, (((0,), (0,)), ((), ())), preferred_element_type=F32)
    preact = preact + bias_ref[...]
    sig = jax.nn.sigmoid(preact)
    hidden_ref[0] = (preact * sig).astype(BF16)
    grad_pre = (cot_ref[0].astype(F32) * sig * (1.0 + preact * (1.0 - sig))).astype(BF16)
    grads = jnp.dot(x, grad_pre, preferred_element_type=F32)
    back = lax.dot_general(
        weight, grad_pre, (((1,), (1,)), ((), ())), preferred_element_type=F32
    )
    bias_sum = jnp.sum(grad_pre.astype(F32), axis=0, keepdims=True)
    half = hid // 2
    tail = split_rows(bias_sum[:, :half], bias_sum[:, half:])
    reps = send_ref.shape[0]
    back_ref[...] = back.reshape(back_ref.shape).astype(BF16)
    send_ref[...] = jnp.concatenate(
        [
            grads[:, :half].reshape(reps, -1, half),
            grads[:, half:].reshape(reps, -1, half),
            jnp.broadcast_to(tail[None], (reps, 8, half)),
        ],
        axis=1,
    ).astype(BF16)


def split_rows(first, second):
    place = lax.broadcasted_iota(jnp.int32, (8, first.shape[1]), 0)
    first_hi = first.astype(BF16).astype(F32)
    second_hi = second.astype(BF16).astype(F32)
    out = jnp.where(place == 0, first_hi, 0.0)
    out = jnp.where(place == 1, second_hi, out)
    out = jnp.where(place == 2, first - first_hi, out)
    return jnp.where(place == 3, second - second_hi, out)


def add_up(parts):
    total = jnp.sum(parts, axis=0)
    rows = total.shape[0] - 8
    low = total[rows:]
    return total[:rows], low[0:1] + low[2:3], low[1:2] + low[3:4]


def rep_sum_kernel(got_ref, back_ref, out_ref):
    total, first, second = add_up(got_ref[...].astype(F32))
    whole = jnp.concatenate([total, split_rows(first, second)], axis=0)
    peers = out_ref.shape[0]
    whole = jnp.broadcast_to(whole[None], (peers,) + whole.shape)
    out_ref[...] = jnp.concatenate([back_ref[...].astype(F32), whole], axis=1).astype(BF16)


def feat_sum_kernel(factor, got_ref, out_ref, bias_ref):
    total, first, second = add_up(got_ref[...].astype(F32)[:, 8:, :])
    bias_ref[...] = factor * jnp.concatenate([first, second], axis=1)
    out_ref[...] = jnp.broadcast_to((factor * total).astype(BF16)[None], out_ref.shape)


def assemble_kernel(got_ref, self_ref, neigh_ref):
    side = got_ref.shape[2]
    got = got_ref[...].astype(F32)
    for h in range(2):
        even = got[:, 16 * h : 16 * h + 8]
        odd = got[:, 16 * h + 8 : 16 * h + 16]
        upper = lax.broadcasted_iota(jnp.int32, even.shape, 1) < 4
        first = jnp.where(upper, even, pltpu.roll(odd, 4, 1))
        second = jnp.where(upper, pltpu.roll(even, 4, 1), odd)
        self_ref[:, h * side : (h + 1) * side] = first.reshape(-1, side)
        neigh_ref[:, h * side : (h + 1) * side] = second.reshape(-1, side)


def backward_kernel(ids_ref, counts_ref, got_ref, adj, out_ref, acc):
    acc[...] = jnp.zeros_like(acc)
    depth, blocks = ids_ref.shape[1], ids_ref.shape[2]
    side = adj.shape[3]
    sources = acc.shape[0] - 1
    for b in range(blocks):
        count = counts_ref[0, b]
        lhs = got_ref[b, 0:16, :]
        contrib = lax.dot_general(
            lhs,
            adj[b].reshape(depth * side, side),
            (((1,), (1,)), ((), ())),
            preferred_element_type=F32,
        )
        for k in range(depth):
            place = jnp.where(k < count, ids_ref[0, k, b], sources)
            acc[place] = acc[place] + contrib[0:8, k * side : (k + 1) * side]
    chans = out_ref.shape[1]
    for n in range(sources):
        total = pltpu.roll(acc[n], 4, 0)
        if n < blocks:
            total = total + got_ref[n, 0:16, :].astype(F32)[0:8]
        out_ref[0, :, n * side : (n + 1) * side] = total[0:chans].astype(BF16)


SMEM = pl.BlockSpec(memory_space=pltpu.SMEM)
VMEM = pl.BlockSpec(memory_space=pltpu.VMEM)
HBM = pl.BlockSpec(memory_space=pl.ANY)


def params(mib):
    return pltpu.CompilerParams(vmem_limit_bytes=mib * 1024 * 1024)


def local(
    feature_table,
    node_ids,
    block_ids,
    block_counts,
    adjacency,
    self_weight,
    neigh_weight,
    bias_vector,
    cotangent,
):
    chans = feature_table.shape[0]
    node_count = node_ids.shape[1]
    blocks, depth, side = adjacency.shape[1:4]
    sources = node_count // side
    peers = lax.axis_size("feat")
    reps = lax.axis_size("rep")
    feats, hid = self_weight.shape
    rows = cotangent.shape[1]
    lists = jnp.transpose(block_ids, (0, 2, 1))
    sent = pl.pallas_call(
        forward_kernel,
        out_shape=jax.ShapeDtypeStruct((peers, 8, side), BF16),
        in_specs=[HBM] * 5,
        out_specs=VMEM,
        scratch_shapes=[
            pltpu.VMEM(adjacency.shape[1:], BF16),
            pltpu.SMEM(lists.shape, jnp.int32),
            pltpu.SMEM(block_counts.shape, jnp.int32),
            pltpu.VMEM(node_ids.shape, jnp.int32),
            pltpu.VMEM(feature_table.shape, BF16),
            pltpu.VMEM((feature_table.shape[1] // LOW * chans, LOW), F32),
            pltpu.VMEM((sources, 8, side), F32),
            pltpu.VMEM((peers, 8, side), F32),
            pltpu.SemaphoreType.DMA((ADJ_PARTS + 4,)),
        ],
        compiler_params=params(FWD_MIB),
        name="forward",
    )(lists, block_counts, node_ids, feature_table, adjacency)
    arrived = lax.all_to_all(sent, "feat", split_axis=0, concat_axis=0, tiled=True)
    hidden, back, send = pl.pallas_call(
        dense_kernel,
        out_shape=(
            jax.ShapeDtypeStruct(cotangent.shape, BF16),
            jax.ShapeDtypeStruct((peers, 8, side), BF16),
            jax.ShapeDtypeStruct((reps, 4 * feats // reps + 8, hid // 2), BF16),
        ),
        in_specs=[VMEM] * 5,
        out_specs=(VMEM, VMEM, VMEM),
        compiler_params=params(16),
        name="dense",
    )(arrived, self_weight, neigh_weight, bias_vector.reshape(1, hid), cotangent)
    over_rep = lax.all_to_all(send, "rep", split_axis=0, concat_axis=0, tiled=True)
    rows_sent = send.shape[1]
    merged = pl.pallas_call(
        rep_sum_kernel,
        out_shape=jax.ShapeDtypeStruct((peers, rows_sent + 8, side), BF16),
        in_specs=[VMEM, VMEM],
        out_specs=VMEM,
        compiler_params=params(8),
        name="rep_sum",
    )(over_rep, back)
    got = lax.all_to_all(merged, "feat", split_axis=0, concat_axis=0, tiled=True)
    factor = float(rows * peers * reps) ** (-0.5)
    pieces, bias_grad = pl.pallas_call(
        lambda *refs: feat_sum_kernel(factor, *refs),
        out_shape=(
            jax.ShapeDtypeStruct((reps, rows_sent - 8, side), BF16),
            jax.ShapeDtypeStruct((1, hid), F32),
        ),
        in_specs=[VMEM],
        out_specs=(VMEM, VMEM),
        compiler_params=params(8),
        name="feat_sum",
    )(got)
    whole = lax.all_to_all(pieces, "rep", split_axis=0, concat_axis=0, tiled=True)
    feature_grad = pl.pallas_call(
        backward_kernel,
        out_shape=jax.ShapeDtypeStruct((1, chans, node_count), BF16),
        in_specs=[SMEM, SMEM, VMEM, VMEM],
        out_specs=VMEM,
        scratch_shapes=[pltpu.VMEM((sources + 1, 8, side), F32)],
        compiler_params=params(16),
        cost_estimate=pl.CostEstimate(
            flops=2 * 16 * adjacency.size, bytes_accessed=2 * adjacency.size, transcendentals=0
        ),
        name="spread_back",
    )(lists, block_counts, got, adjacency.reshape(adjacency.shape[1:]))
    self_grad, neigh_grad = pl.pallas_call(
        assemble_kernel,
        out_shape=(
            jax.ShapeDtypeStruct((feats, hid), F32),
            jax.ShapeDtypeStruct((feats, hid), F32),
        ),
        in_specs=[VMEM],
        out_specs=(VMEM, VMEM),
        compiler_params=params(8),
        name="assemble",
    )(whole)
    return hidden, feature_grad, self_grad, neigh_grad, bias_grad.reshape(hid)


def solution(mesh):
    return jax.shard_map(
        local,
        mesh=mesh,
        in_specs=(
            P("feat", None),
            P("rep", None),
            P("rep", None, None),
            P("rep", None),
            P("rep", None, None, None, None),
            P(),
            P(),
            P(),
            P("rep", "feat", None),
        ),
        out_specs=(P("rep", "feat", None), P("rep", "feat", None), P(), P(), P()),
        check_vma=False,
    )
```

```python
import jax
import jax.numpy as jnp
from jax import lax
from jax.experimental import pallas as pl
from jax.experimental.pallas import tpu as pltpu
from jax.sharding import PartitionSpec as P

F32 = jnp.float32
BF16 = jnp.bfloat16
ADJ_PARTS = 8
LOW = 256
CHUNK = 512
FWD_MIB = 58


def forward_kernel(
    lists_hbm,
    counts_hbm,
    nodes_hbm,
    table_hbm,
    adj_hbm,
    out_ref,
    adj,
    ids_ref,
    counts_ref,
    nodes_ref,
    table_ref,
    rows_f32,
    feats,
    staged,
    sems,
):
    per = adj.shape[0] // ADJ_PARTS
    inputs = [
        pltpu.make_async_copy(table_hbm, table_ref, sems.at[ADJ_PARTS]),
        pltpu.make_async_copy(nodes_hbm, nodes_ref, sems.at[ADJ_PARTS + 1]),
    ]
    lists = [
        pltpu.make_async_copy(lists_hbm, ids_ref, sems.at[ADJ_PARTS + 2]),
        pltpu.make_async_copy(counts_hbm, counts_ref, sems.at[ADJ_PARTS + 3]),
    ]
    copies = [
        pltpu.make_async_copy(
            adj_hbm.at[0, pl.ds(p * per, per)], adj.at[pl.ds(p * per, per)], sems.at[p]
        )
        for p in range(ADJ_PARTS)
    ]
    for copy in inputs + lists + copies:
        copy.start()
    for copy in inputs:
        copy.wait()
    chans = table_ref.shape[0]
    groups = table_ref.shape[1] // LOW
    for q in range(groups):
        rows_f32[q * chans : (q + 1) * chans, :] = table_ref[:, q * LOW : (q + 1) * LOW].astype(F32)
    table_rows = rows_f32[...].astype(BF16)
    node_count = nodes_ref.shape[1]
    for start in range(0, node_count, CHUNK):
        ids = nodes_ref[:, start : start + CHUNK]
        low = ids & (LOW - 1)
        high = ids // LOW
        onehot = jnp.where(lax.broadcasted_iota(jnp.int32, (LOW, CHUNK), 0) == low, 1.0, 0.0)
        spread = jnp.dot(table_rows, onehot.astype(BF16), preferred_element_type=F32)
        group = lax.broadcasted_iota(jnp.int32, spread.shape, 0) // chans
        kept = jnp.where(group == high, spread, 0.0)
        two = jnp.sum(kept.reshape(-1, 8, CHUNK), axis=0)
        both = two + pltpu.roll(two, 4, 0)
        for j in range(CHUNK // 128):
            feats[start // 128 + j] = both[:, j * 128 : (j + 1) * 128]
    for copy in lists:
        copy.wait()
    depth, blocks = ids_ref.shape[1], ids_ref.shape[2]
    side = adj.shape[3]
    upper = lax.broadcasted_iota(jnp.int32, (8, side), 0) < chans
    for b in range(blocks):
        if b % per == 0:
            copies[b // per].wait()
        count = counts_ref[0, b]
        picked = [
            jnp.where(k < count, feats[ids_ref[0, k, b]], 0.0) for k in range(depth)
        ]
        lhs = jnp.concatenate(picked, axis=1).astype(BF16)
        agg = jnp.dot(lhs, adj[b].reshape(depth * side, side), preferred_element_type=F32)
        staged[b] = jnp.where(upper, feats[b], agg)
    out_ref[...] = staged[...].astype(BF16)


def dense_kernel(x_ref, sw_ref, nw_ref, bias_ref, cot_ref, hidden_ref, send_ref):
    feats = sw_ref.shape[0]
    hid = sw_ref.shape[1]
    sw = sw_ref[...].astype(F32).reshape(feats // 8, 8, hid)
    nw = nw_ref[...].astype(F32).reshape(feats // 8, 8, hid)
    upper = lax.broadcasted_iota(jnp.int32, sw.shape, 1) < 4
    even = jnp.where(upper, sw, pltpu.roll(nw, 4, 1))
    odd = jnp.where(upper, pltpu.roll(sw, 4, 1), nw)
    weight = jnp.concatenate([even, odd], axis=1).reshape(2 * feats, hid).astype(BF16)
    rows = x_ref.shape[2]
    x = x_ref[...].reshape(2 * feats, rows)
    preact = lax.dot_general(x, weight, (((0,), (0,)), ((), ())), preferred_element_type=F32)
    preact = preact + bias_ref[...]
    sig = jax.nn.sigmoid(preact)
    hidden_ref[0] = (preact * sig).astype(BF16)
    grad_pre = (cot_ref[0].astype(F32) * sig * (1.0 + preact * (1.0 - sig))).astype(BF16)
    grads = jnp.dot(x, grad_pre, preferred_element_type=F32)
    back = lax.dot_general(
        weight, grad_pre, (((1,), (1,)), ((), ())), preferred_element_type=F32
    )
    bias_sum = jnp.sum(grad_pre.astype(F32), axis=0, keepdims=True)
    half = hid // 2
    tail = split_rows(bias_sum[:, :half], bias_sum[:, half:])
    peers = send_ref.shape[0]
    send_ref[...] = jnp.concatenate(
        [
            back.reshape(peers, 8, rows),
            grads[:, :half].reshape(peers, 8, half),
            grads[:, half:].reshape(peers, 8, half),
            jnp.broadcast_to(tail[None], (peers, 8, half)),
        ],
        axis=1,
    ).astype(BF16)


def split_rows(first, second):
    place = lax.broadcasted_iota(jnp.int32, (8, first.shape[1]), 0)
    first_hi = first.astype(BF16).astype(F32)
    second_hi = second.astype(BF16).astype(F32)
    out = jnp.where(place == 0, first_hi, 0.0)
    out = jnp.where(place == 1, second_hi, out)
    out = jnp.where(place == 2, first - first_hi, out)
    return jnp.where(place == 3, second - second_hi, out)


def add_up(parts):
    total = jnp.sum(parts, axis=0)
    rows = total.shape[0] - 8
    low = total[rows:]
    return total[:rows], low[0:1] + low[2:3], low[1:2] + low[3:4]


def feat_sum_kernel(got_ref, out_ref):
    total, first, second = add_up(got_ref[...].astype(F32)[:, 8:, :])
    whole = jnp.concatenate([total, split_rows(first, second)], axis=0).astype(BF16)
    out_ref[...] = jnp.broadcast_to(whole[None], out_ref.shape)


def rep_sum_kernel(factor, got_ref, out_ref, bias_ref):
    total, first, second = add_up(got_ref[...].astype(F32))
    bias_ref[...] = factor * jnp.concatenate([first, second], axis=1)
    out_ref[...] = jnp.broadcast_to((factor * total).astype(BF16)[None], out_ref.shape)


def assemble_kernel(got_ref, self_ref, neigh_ref):
    peers, _, side = got_ref.shape
    got = got_ref[...].astype(F32).reshape(peers // 2, 32, side)
    for h in range(2):
        even = got[:, 8 * h : 8 * h + 8]
        odd = got[:, 16 + 8 * h : 24 + 8 * h]
        upper = lax.broadcasted_iota(jnp.int32, even.shape, 1) < 4
        first = jnp.where(upper, even, pltpu.roll(odd, 4, 1))
        second = jnp.where(upper, pltpu.roll(even, 4, 1), odd)
        self_ref[:, h * side : (h + 1) * side] = first.reshape(-1, side)
        neigh_ref[:, h * side : (h + 1) * side] = second.reshape(-1, side)


def backward_kernel(ids_ref, counts_ref, got_ref, adj, out_ref, acc):
    acc[...] = jnp.zeros_like(acc)
    depth, blocks = ids_ref.shape[1], ids_ref.shape[2]
    side = adj.shape[3]
    sources = acc.shape[0] - 1
    for b in range(blocks):
        count = counts_ref[0, b]
        lhs = got_ref[b, 0:16, :]
        contrib = lax.dot_general(
            lhs,
            adj[b].reshape(depth * side, side),
            (((1,), (1,)), ((), ())),
            preferred_element_type=F32,
        )
        for k in range(depth):
            place = jnp.where(k < count, ids_ref[0, k, b], sources)
            acc[place] = acc[place] + contrib[0:8, k * side : (k + 1) * side]
    chans = out_ref.shape[1]
    for n in range(sources):
        total = pltpu.roll(acc[n], 4, 0)
        if n < blocks:
            total = total + got_ref[n, 0:16, :].astype(F32)[0:8]
        out_ref[0, :, n * side : (n + 1) * side] = total[0:chans].astype(BF16)


SMEM = pl.BlockSpec(memory_space=pltpu.SMEM)
VMEM = pl.BlockSpec(memory_space=pltpu.VMEM)
HBM = pl.BlockSpec(memory_space=pl.ANY)


def params(mib):
    return pltpu.CompilerParams(vmem_limit_bytes=mib * 1024 * 1024)


def local(
    feature_table,
    node_ids,
    block_ids,
    block_counts,
    adjacency,
    self_weight,
    neigh_weight,
    bias_vector,
    cotangent,
):
    chans = feature_table.shape[0]
    node_count = node_ids.shape[1]
    blocks, depth, side = adjacency.shape[1:4]
    sources = node_count // side
    peers = lax.axis_size("feat")
    reps = lax.axis_size("rep")
    feats, hid = self_weight.shape
    rows = cotangent.shape[1]
    lists = jnp.transpose(block_ids, (0, 2, 1))
    sent = pl.pallas_call(
        forward_kernel,
        out_shape=jax.ShapeDtypeStruct((peers, 8, side), BF16),
        in_specs=[HBM] * 5,
        out_specs=VMEM,
        scratch_shapes=[
            pltpu.VMEM(adjacency.shape[1:], BF16),
            pltpu.SMEM(lists.shape, jnp.int32),
            pltpu.SMEM(block_counts.shape, jnp.int32),
            pltpu.VMEM(node_ids.shape, jnp.int32),
            pltpu.VMEM(feature_table.shape, BF16),
            pltpu.VMEM((feature_table.shape[1] // LOW * chans, LOW), F32),
            pltpu.VMEM((sources, 8, side), F32),
            pltpu.VMEM((peers, 8, side), F32),
            pltpu.SemaphoreType.DMA((ADJ_PARTS + 4,)),
        ],
        compiler_params=params(FWD_MIB),
        name="forward",
    )(lists, block_counts, node_ids, feature_table, adjacency)
    arrived = lax.all_to_all(sent, "feat", split_axis=0, concat_axis=0, tiled=True)
    hidden, send = pl.pallas_call(
        dense_kernel,
        out_shape=(
            jax.ShapeDtypeStruct(cotangent.shape, BF16),
            jax.ShapeDtypeStruct((peers, 32, side), BF16),
        ),
        in_specs=[VMEM] * 5,
        out_specs=(VMEM, VMEM),
        compiler_params=params(16),
        name="dense",
    )(arrived, self_weight, neigh_weight, bias_vector.reshape(1, hid), cotangent)
    got = lax.all_to_all(send, "feat", split_axis=0, concat_axis=0, tiled=True)
    partial = pl.pallas_call(
        feat_sum_kernel,
        out_shape=jax.ShapeDtypeStruct((reps, 24, side), BF16),
        in_specs=[VMEM],
        out_specs=VMEM,
        compiler_params=params(8),
        name="feat_sum",
    )(got)
    over_rep = lax.all_to_all(partial, "rep", split_axis=0, concat_axis=0, tiled=True)
    factor = float(rows * peers * reps) ** (-0.5)
    pieces, bias_grad = pl.pallas_call(
        lambda *refs: rep_sum_kernel(factor, *refs),
        out_shape=(
            jax.ShapeDtypeStruct((peers, 16, side), BF16),
            jax.ShapeDtypeStruct((1, hid), F32),
        ),
        in_specs=[VMEM],
        out_specs=(VMEM, VMEM),
        compiler_params=params(8),
        name="rep_sum",
    )(over_rep)
    whole = lax.all_to_all(pieces, "feat", split_axis=0, concat_axis=0, tiled=True)
    feature_grad = pl.pallas_call(
        backward_kernel,
        out_shape=jax.ShapeDtypeStruct((1, chans, node_count), BF16),
        in_specs=[SMEM, SMEM, VMEM, VMEM],
        out_specs=VMEM,
        scratch_shapes=[pltpu.VMEM((sources + 1, 8, side), F32)],
        compiler_params=params(16),
        cost_estimate=pl.CostEstimate(
            flops=2 * 16 * adjacency.size, bytes_accessed=2 * adjacency.size, transcendentals=0
        ),
        name="spread_back",
    )(lists, block_counts, got, adjacency.reshape(adjacency.shape[1:]))
    self_grad, neigh_grad = pl.pallas_call(
        assemble_kernel,
        out_shape=(
            jax.ShapeDtypeStruct((feats, hid), F32),
            jax.ShapeDtypeStruct((feats, hid), F32),
        ),
        in_specs=[VMEM],
        out_specs=(VMEM, VMEM),
        compiler_params=params(8),
        name="assemble",
    )(whole)
    return hidden, feature_grad, self_grad, neigh_grad, bias_grad.reshape(hid)


def solution(mesh):
    return jax.shard_map(
        local,
        mesh=mesh,
        in_specs=(
            P("feat", None),
            P("rep", None),
            P("rep", None, None),
            P("rep", None),
            P("rep", None, None, None, None),
            P(),
            P(),
            P(),
            P("rep", "feat", None),
        ),
        out_specs=(P("rep", "feat", None), P("rep", "feat", None), P(), P(), P()),
        check_vma=False,
    )
```

```python
import jax
import jax.numpy as jnp
from jax import lax
from jax.experimental import pallas as pl
from jax.experimental.pallas import tpu as pltpu
from jax.sharding import PartitionSpec as P

F32 = jnp.float32
BF16 = jnp.bfloat16
ADJ_PARTS = 8
LOW = 256
CHUNK = 512


def adj_copies(adj_hbm, adj, sems):
    per = adj.shape[0] // ADJ_PARTS
    return per, [
        pltpu.make_async_copy(
            adj_hbm.at[0, pl.ds(p * per, per)], adj.at[pl.ds(p * per, per)], sems.at[p]
        )
        for p in range(ADJ_PARTS)
    ]


def forward_kernel(
    lists_hbm,
    counts_hbm,
    nodes_hbm,
    table_hbm,
    adj_hbm,
    out_ref,
    adj,
    ids_ref,
    counts_ref,
    nodes_ref,
    table_ref,
    rows_f32,
    feats,
    staged,
    sems,
):
    per, copies = adj_copies(adj_hbm, adj, sems)
    inputs = [
        pltpu.make_async_copy(table_hbm, table_ref, sems.at[ADJ_PARTS]),
        pltpu.make_async_copy(nodes_hbm, nodes_ref, sems.at[ADJ_PARTS + 1]),
    ]
    lists = [
        pltpu.make_async_copy(lists_hbm, ids_ref, sems.at[ADJ_PARTS + 2]),
        pltpu.make_async_copy(counts_hbm, counts_ref, sems.at[ADJ_PARTS + 3]),
    ]
    for copy in inputs + lists + copies:
        copy.start()
    for copy in inputs:
        copy.wait()
    chans = table_ref.shape[0]
    groups = table_ref.shape[1] // LOW
    for q in range(groups):
        rows_f32[q * chans : (q + 1) * chans, :] = table_ref[:, q * LOW : (q + 1) * LOW].astype(F32)
    table_rows = rows_f32[...].astype(BF16)
    node_count = nodes_ref.shape[1]
    column = lax.broadcasted_iota(jnp.int32, (LOW, CHUNK), 0).astype(F32).astype(BF16)
    one = jnp.ones((LOW, CHUNK), BF16)
    zero = jnp.zeros((LOW, CHUNK), BF16)
    for start in range(0, node_count, CHUNK):
        ids = nodes_ref[:, start : start + CHUNK]
        low = ids & (LOW - 1)
        high = ids // LOW
        onehot = jnp.where(column == low.astype(F32).astype(BF16), one, zero)
        spread = jnp.dot(table_rows, onehot, preferred_element_type=F32)
        group = lax.broadcasted_iota(jnp.int32, spread.shape, 0) // chans
        kept = jnp.where(group == high, spread, 0.0)
        two = jnp.sum(kept.reshape(-1, 8, CHUNK), axis=0)
        both = two + pltpu.roll(two, 4, 0)
        for j in range(CHUNK // 128):
            feats[start // 128 + j] = both[:, j * 128 : (j + 1) * 128]
    for copy in lists:
        copy.wait()
    depth, blocks = ids_ref.shape[1], ids_ref.shape[2]
    side = adj.shape[3]
    upper = lax.broadcasted_iota(jnp.int32, (8, side), 0) < chans
    for b in range(blocks):
        if b % per == 0:
            copies[b // per].wait()
        count = counts_ref[0, b]
        picked = [
            jnp.where(k < count, feats[ids_ref[0, k, b]], 0.0) for k in range(depth)
        ]
        lhs = jnp.concatenate(picked, axis=1).astype(BF16)
        agg = jnp.dot(lhs, adj[b].reshape(depth * side, side), preferred_element_type=F32)
        staged[b] = jnp.where(upper, feats[b], agg)
    out_ref[...] = staged[...].astype(BF16)


def dense_kernel(x_ref, sw_ref, nw_ref, bias_ref, cot_ref, hidden_ref, send_ref):
    feats = sw_ref.shape[0]
    hid = sw_ref.shape[1]
    sw = sw_ref[...].astype(F32).reshape(feats // 8, 8, hid)
    nw = nw_ref[...].astype(F32).reshape(feats // 8, 8, hid)
    upper = lax.broadcasted_iota(jnp.int32, sw.shape, 1) < 4
    even = jnp.where(upper, sw, pltpu.roll(nw, 4, 1))
    odd = jnp.where(upper, pltpu.roll(sw, 4, 1), nw)
    weight = jnp.concatenate([even, odd], axis=1).reshape(2 * feats, hid).astype(BF16)
    rows = x_ref.shape[2]
    x = x_ref[...].reshape(2 * feats, rows)
    preact = lax.dot_general(x, weight, (((0,), (0,)), ((), ())), preferred_element_type=F32)
    preact = preact + bias_ref[...]
    sig = jax.nn.sigmoid(preact)
    hidden_ref[0] = (preact * sig).astype(BF16)
    grad_pre = (cot_ref[0].astype(F32) * sig * (1.0 + preact * (1.0 - sig))).astype(BF16)
    grads = jnp.dot(x, grad_pre, preferred_element_type=F32)
    back = lax.dot_general(
        weight, grad_pre, (((1,), (1,)), ((), ())), preferred_element_type=F32
    )
    bias_sum = jnp.sum(grad_pre.astype(F32), axis=0, keepdims=True)
    half = hid // 2
    tail = split_rows(bias_sum[:, :half], bias_sum[:, half:])
    peers = send_ref.shape[0]
    send_ref[...] = jnp.concatenate(
        [
            back.reshape(peers, 8, rows),
            grads[:, :half].reshape(peers, 8, half),
            grads[:, half:].reshape(peers, 8, half),
            jnp.broadcast_to(tail[None], (peers, 8, half)),
        ],
        axis=1,
    ).astype(BF16)


def split_rows(first, second):
    place = lax.broadcasted_iota(jnp.int32, (8, first.shape[1]), 0)
    first_hi = first.astype(BF16).astype(F32)
    second_hi = second.astype(BF16).astype(F32)
    out = jnp.where(place == 0, first_hi, 0.0)
    out = jnp.where(place == 1, second_hi, out)
    out = jnp.where(place == 2, first - first_hi, out)
    return jnp.where(place == 3, second - second_hi, out)


def add_up(parts):
    total = jnp.sum(parts, axis=0)
    rows = total.shape[0] - 8
    low = total[rows:]
    return total[:rows], low[0:1] + low[2:3], low[1:2] + low[3:4]


def feat_sum_kernel(got_ref, out_ref):
    total, first, second = add_up(got_ref[...].astype(F32)[:, 8:, :])
    whole = jnp.concatenate([total, split_rows(first, second)], axis=0).astype(BF16)
    out_ref[...] = jnp.broadcast_to(whole[None], out_ref.shape)


def rep_sum_kernel(factor, got_ref, out_ref, bias_ref):
    total, first, second = add_up(got_ref[...].astype(F32))
    bias_ref[...] = factor * jnp.concatenate([first, second], axis=1)
    out_ref[...] = jnp.broadcast_to((factor * total).astype(BF16)[None], out_ref.shape)


def assemble_kernel(got_ref, self_ref, neigh_ref):
    peers, _, side = got_ref.shape
    got = got_ref[...].astype(F32).reshape(peers // 2, 32, side)
    for h in range(2):
        even = got[:, 8 * h : 8 * h + 8]
        odd = got[:, 16 + 8 * h : 24 + 8 * h]
        upper = lax.broadcasted_iota(jnp.int32, even.shape, 1) < 4
        first = jnp.where(upper, even, pltpu.roll(odd, 4, 1))
        second = jnp.where(upper, pltpu.roll(even, 4, 1), odd)
        self_ref[:, h * side : (h + 1) * side] = first.reshape(-1, side)
        neigh_ref[:, h * side : (h + 1) * side] = second.reshape(-1, side)


def backward_kernel(
    ids_ref, counts_ref, got_ref, hid_ref, adj_hbm, out_ref, hidden_ref, adj, acc, sems
):
    per, copies = adj_copies(adj_hbm, adj, sems)
    for copy in copies:
        copy.start()
    hidden_ref[...] = hid_ref[...]
    acc[...] = jnp.zeros_like(acc)
    depth, blocks = ids_ref.shape[1], ids_ref.shape[2]
    side = adj.shape[3]
    sources = acc.shape[0] - 1
    for b in range(blocks):
        if b % per == 0:
            copies[b // per].wait()
        count = counts_ref[0, b]
        lhs = got_ref[b, 0:16, :]
        contrib = lax.dot_general(
            lhs,
            adj[b].reshape(depth * side, side),
            (((1,), (1,)), ((), ())),
            preferred_element_type=F32,
        )
        for k in range(depth):
            place = jnp.where(k < count, ids_ref[0, k, b], sources)
            acc[place] = acc[place] + contrib[0:8, k * side : (k + 1) * side]
    chans = out_ref.shape[1]
    for n in range(sources):
        total = pltpu.roll(acc[n], 4, 0)
        if n < blocks:
            total = total + got_ref[n, 0:16, :].astype(F32)[0:8]
        out_ref[0, :, n * side : (n + 1) * side] = total[0:chans].astype(BF16)


SMEM = pl.BlockSpec(memory_space=pltpu.SMEM)
VMEM = pl.BlockSpec(memory_space=pltpu.VMEM)
HBM = pl.BlockSpec(memory_space=pl.ANY)


def in_hbm(array):
    return pltpu.with_memory_space_constraint(array, pltpu.HBM)


def params(mib):
    return pltpu.CompilerParams(vmem_limit_bytes=mib * 1024 * 1024)


def local(
    feature_table,
    node_ids,
    block_ids,
    block_counts,
    adjacency,
    self_weight,
    neigh_weight,
    bias_vector,
    cotangent,
):
    chans = feature_table.shape[0]
    node_count = node_ids.shape[1]
    blocks, depth, side = adjacency.shape[1:4]
    sources = node_count // side
    peers = lax.axis_size("feat")
    reps = lax.axis_size("rep")
    feats, hid = self_weight.shape
    rows = cotangent.shape[1]
    lists = jnp.transpose(block_ids, (0, 2, 1))
    sent = pl.pallas_call(
        forward_kernel,
        out_shape=jax.ShapeDtypeStruct((peers, 8, side), BF16),
        in_specs=[HBM] * 5,
        out_specs=VMEM,
        scratch_shapes=[
            pltpu.VMEM(adjacency.shape[1:], BF16),
            pltpu.SMEM(lists.shape, jnp.int32),
            pltpu.SMEM(block_counts.shape, jnp.int32),
            pltpu.VMEM(node_ids.shape, jnp.int32),
            pltpu.VMEM(feature_table.shape, BF16),
            pltpu.VMEM((feature_table.shape[1] // LOW * chans, LOW), F32),
            pltpu.VMEM((sources, 8, side), F32),
            pltpu.VMEM((peers, 8, side), F32),
            pltpu.SemaphoreType.DMA((ADJ_PARTS + 4,)),
        ],
        compiler_params=params(24),
        name="forward",
    )(*[in_hbm(v) for v in (lists, block_counts, node_ids, feature_table, adjacency)])
    arrived = lax.all_to_all(sent, "feat", split_axis=0, concat_axis=0, tiled=True)
    hid_vmem, send = pl.pallas_call(
        dense_kernel,
        out_shape=(
            jax.ShapeDtypeStruct(cotangent.shape, BF16),
            jax.ShapeDtypeStruct((peers, 32, side), BF16),
        ),
        in_specs=[VMEM] * 5,
        out_specs=(VMEM, VMEM),
        compiler_params=params(16),
        name="dense",
    )(arrived, self_weight, neigh_weight, bias_vector.reshape(1, hid), cotangent)
    got = lax.all_to_all(send, "feat", split_axis=0, concat_axis=0, tiled=True)
    partial = pl.pallas_call(
        feat_sum_kernel,
        out_shape=jax.ShapeDtypeStruct((reps, 24, side), BF16),
        in_specs=[VMEM],
        out_specs=VMEM,
        compiler_params=params(8),
        name="feat_sum",
    )(got)
    over_rep = lax.all_to_all(partial, "rep", split_axis=0, concat_axis=0, tiled=True)
    factor = float(rows * peers * reps) ** (-0.5)
    pieces, bias_grad = pl.pallas_call(
        lambda *refs: rep_sum_kernel(factor, *refs),
        out_shape=(
            jax.ShapeDtypeStruct((peers, 16, side), BF16),
            jax.ShapeDtypeStruct((1, hid), F32),
        ),
        in_specs=[VMEM],
        out_specs=(VMEM, VMEM),
        compiler_params=params(8),
        name="rep_sum",
    )(over_rep)
    whole = lax.all_to_all(pieces, "feat", split_axis=0, concat_axis=0, tiled=True)
    feature_grad, hidden = pl.pallas_call(
        backward_kernel,
        out_shape=(
            jax.ShapeDtypeStruct((1, chans, node_count), BF16),
            jax.ShapeDtypeStruct(cotangent.shape, BF16),
        ),
        in_specs=[SMEM, SMEM, VMEM, VMEM, HBM],
        out_specs=(VMEM, VMEM),
        scratch_shapes=[
            pltpu.VMEM(adjacency.shape[1:], BF16),
            pltpu.VMEM((sources + 1, 8, side), F32),
            pltpu.SemaphoreType.DMA((ADJ_PARTS,)),
        ],
        compiler_params=params(24),
        cost_estimate=pl.CostEstimate(
            flops=2 * 16 * adjacency.size, bytes_accessed=2 * adjacency.size, transcendentals=0
        ),
        name="spread_back",
    )(lists, block_counts, got, hid_vmem, in_hbm(adjacency))
    self_grad, neigh_grad = pl.pallas_call(
        assemble_kernel,
        out_shape=(
            jax.ShapeDtypeStruct((feats, hid), F32),
            jax.ShapeDtypeStruct((feats, hid), F32),
        ),
        in_specs=[VMEM],
        out_specs=(VMEM, VMEM),
        compiler_params=params(8),
        name="assemble",
    )(whole)
    return hidden, feature_grad, self_grad, neigh_grad, bias_grad.reshape(hid)


def solution(mesh):
    return jax.shard_map(
        local,
        mesh=mesh,
        in_specs=(
            P("feat", None),
            P("rep", None),
            P("rep", None, None),
            P("rep", None),
            P("rep", None, None, None, None),
            P(),
            P(),
            P(),
            P("rep", "feat", None),
        ),
        out_specs=(P("rep", "feat", None), P("rep", "feat", None), P(), P(), P()),
        check_vma=False,
    )
```

```python
import jax
import jax.numpy as jnp
from jax import lax
from jax.experimental import pallas as pl
from jax.experimental.pallas import tpu as pltpu
from jax.sharding import PartitionSpec as P

F32 = jnp.float32
BF16 = jnp.bfloat16
ADJ_PARTS = 2
LOW = 256
CHUNK = 512


def adj_copies(adj_hbm, adj, sems):
    per = adj.shape[0] // ADJ_PARTS
    return per, [
        pltpu.make_async_copy(
            adj_hbm.at[0, pl.ds(p * per, per)], adj.at[pl.ds(p * per, per)], sems.at[p]
        )
        for p in range(ADJ_PARTS)
    ]


def forward_kernel(
    lists_hbm,
    counts_hbm,
    nodes_hbm,
    table_hbm,
    adj_hbm,
    out_ref,
    adj,
    ids_ref,
    counts_ref,
    nodes_ref,
    table_ref,
    rows_f32,
    feats,
    staged,
    sems,
):
    per, copies = adj_copies(adj_hbm, adj, sems)
    inputs = [
        pltpu.make_async_copy(table_hbm, table_ref, sems.at[ADJ_PARTS]),
        pltpu.make_async_copy(nodes_hbm, nodes_ref, sems.at[ADJ_PARTS + 1]),
    ]
    lists = [
        pltpu.make_async_copy(lists_hbm, ids_ref, sems.at[ADJ_PARTS + 2]),
        pltpu.make_async_copy(counts_hbm, counts_ref, sems.at[ADJ_PARTS + 3]),
    ]
    for copy in inputs + lists + copies:
        copy.start()
    for copy in inputs:
        copy.wait()
    chans = table_ref.shape[0]
    groups = table_ref.shape[1] // LOW
    for q in range(groups):
        rows_f32[q * chans : (q + 1) * chans, :] = table_ref[:, q * LOW : (q + 1) * LOW].astype(F32)
    table_rows = rows_f32[...].astype(BF16)
    node_count = nodes_ref.shape[1]
    column = lax.broadcasted_iota(jnp.int32, (LOW, CHUNK), 0).astype(F32).astype(BF16)
    one = jnp.ones((LOW, CHUNK), BF16)
    zero = jnp.zeros((LOW, CHUNK), BF16)
    for start in range(0, node_count, CHUNK):
        ids = nodes_ref[:, start : start + CHUNK]
        low = ids & (LOW - 1)
        high = ids // LOW
        onehot = jnp.where(column == low.astype(F32).astype(BF16), one, zero)
        spread = jnp.dot(table_rows, onehot, preferred_element_type=F32)
        group = lax.broadcasted_iota(jnp.int32, spread.shape, 0) // chans
        kept = jnp.where(group == high, spread, 0.0)
        two = jnp.sum(kept.reshape(-1, 8, CHUNK), axis=0)
        both = two + pltpu.roll(two, 4, 0)
        for j in range(CHUNK // 128):
            feats[start // 128 + j] = both[:, j * 128 : (j + 1) * 128]
    for copy in lists:
        copy.wait()
    depth, blocks = ids_ref.shape[1], ids_ref.shape[2]
    side = adj.shape[3]
    upper = lax.broadcasted_iota(jnp.int32, (8, side), 0) < chans
    for b in range(blocks):
        if b % per == 0:
            copies[b // per].wait()
        count = counts_ref[0, b]
        picked = [
            jnp.where(k < count, feats[ids_ref[0, k, b]], 0.0) for k in range(depth)
        ]
        lhs = jnp.concatenate(picked, axis=1).astype(BF16)
        agg = jnp.dot(lhs, adj[b].reshape(depth * side, side), preferred_element_type=F32)
        staged[b] = jnp.where(upper, feats[b], agg)
    out_ref[...] = staged[...].astype(BF16)


def dense_kernel(x_ref, sw_ref, nw_ref, bias_ref, cot_ref, hidden_ref, send_ref):
    feats = sw_ref.shape[0]
    hid = sw_ref.shape[1]
    sw = sw_ref[...].astype(F32).reshape(feats // 8, 8, hid)
    nw = nw_ref[...].astype(F32).reshape(feats // 8, 8, hid)
    upper = lax.broadcasted_iota(jnp.int32, sw.shape, 1) < 4
    even = jnp.where(upper, sw, pltpu.roll(nw, 4, 1))
    odd = jnp.where(upper, pltpu.roll(sw, 4, 1), nw)
    weight = jnp.concatenate([even, odd], axis=1).reshape(2 * feats, hid).astype(BF16)
    rows = x_ref.shape[2]
    x = x_ref[...].reshape(2 * feats, rows)
    preact = lax.dot_general(x, weight, (((0,), (0,)), ((), ())), preferred_element_type=F32)
    preact = preact + bias_ref[...]
    sig = jax.nn.sigmoid(preact)
    hidden_ref[0] = (preact * sig).astype(BF16)
    grad_pre = (cot_ref[0].astype(F32) * sig * (1.0 + preact * (1.0 - sig))).astype(BF16)
    grads = jnp.dot(x, grad_pre, preferred_element_type=F32)
    back = lax.dot_general(
        weight, grad_pre, (((1,), (1,)), ((), ())), preferred_element_type=F32
    )
    bias_sum = jnp.sum(grad_pre.astype(F32), axis=0, keepdims=True)
    half = hid // 2
    tail = split_rows(bias_sum[:, :half], bias_sum[:, half:])
    peers = send_ref.shape[0]
    values = [back.reshape(peers, 8, rows)]
    values += [grads[:, at : at + half].reshape(peers, 8, half) for at in (0, half)]
    parts = [v[:, at : at + 4] for v in values for at in (0, 4)]
    parts.append(jnp.broadcast_to(tail[None], (peers, 4, half)))
    send_ref[...] = jnp.concatenate(parts, axis=2).astype(BF16)


def split_rows(first, second):
    place = lax.broadcasted_iota(jnp.int32, (4, first.shape[1]), 0)
    first_hi = first.astype(BF16).astype(F32)
    second_hi = second.astype(BF16).astype(F32)
    out = jnp.where(place == 0, first_hi, 0.0)
    out = jnp.where(place == 1, second_hi, out)
    out = jnp.where(place == 2, first - first_hi, out)
    return jnp.where(place == 3, second - second_hi, out)


def add_up(parts):
    total = jnp.sum(parts, axis=0)
    cols = total.shape[1] - 128
    low = total[:, cols:]
    return total[:, :cols], low[0:1] + low[2:3], low[1:2] + low[3:4]


def feat_sum_kernel(got_ref, out_ref):
    total, first, second = add_up(got_ref[...].astype(F32)[:, :, 256:])
    whole = jnp.concatenate([total, split_rows(first, second)], axis=1).astype(BF16)
    out_ref[...] = jnp.broadcast_to(whole[None], out_ref.shape)


def rep_sum_kernel(factor, got_ref, out_ref, bias_ref):
    total, first, second = add_up(got_ref[...].astype(F32))
    bias_ref[...] = factor * jnp.concatenate([first, second], axis=1)
    out_ref[...] = jnp.broadcast_to((factor * total).astype(BF16)[None], out_ref.shape)


def assemble_kernel(got_ref, self_ref, neigh_ref):
    got = got_ref[...].astype(F32)
    side = got.shape[2] // 4
    for h in range(2):
        for j, out_ref in enumerate((self_ref, neigh_ref)):
            at = (2 * h + j) * side
            out_ref[:, h * side : (h + 1) * side] = got[:, :, at : at + side].reshape(-1, side)


def backward_kernel(
    ids_ref, counts_ref, got_ref, hid_ref, adj_hbm, out_ref, hidden_ref, adj, acc, sems
):
    per, copies = adj_copies(adj_hbm, adj, sems)
    for copy in copies:
        copy.start()
    hidden_ref[...] = hid_ref[...]
    acc[...] = jnp.zeros_like(acc)
    depth, blocks = ids_ref.shape[1], ids_ref.shape[2]
    side = adj.shape[3]
    sources = acc.shape[0] - 1
    for b in range(blocks):
        if b % per == 0:
            copies[b // per].wait()
        count = counts_ref[0, b]
        lhs = got_ref[b, :, side : 2 * side]
        contrib = lax.dot_general(
            lhs,
            adj[b].reshape(depth * side, side),
            (((1,), (1,)), ((), ())),
            preferred_element_type=F32,
        )
        for k in range(depth):
            place = jnp.where(k < count, ids_ref[0, k, b], sources)
            acc[place] = acc[place] + contrib[:, k * side : (k + 1) * side]
    for n in range(sources):
        total = acc[n]
        if n < blocks:
            total = total + got_ref[n, :, 0:side].astype(F32)
        out_ref[0, :, n * side : (n + 1) * side] = total.astype(BF16)


SMEM = pl.BlockSpec(memory_space=pltpu.SMEM)
VMEM = pl.BlockSpec(memory_space=pltpu.VMEM)
HBM = pl.BlockSpec(memory_space=pl.ANY)


def in_hbm(array):
    return pltpu.with_memory_space_constraint(array, pltpu.HBM)


def params(mib):
    return pltpu.CompilerParams(vmem_limit_bytes=mib * 1024 * 1024)


def local(
    feature_table,
    node_ids,
    block_ids,
    block_counts,
    adjacency,
    self_weight,
    neigh_weight,
    bias_vector,
    cotangent,
):
    chans = feature_table.shape[0]
    node_count = node_ids.shape[1]
    blocks, depth, side = adjacency.shape[1:4]
    sources = node_count // side
    peers = lax.axis_size("feat")
    reps = lax.axis_size("rep")
    feats, hid = self_weight.shape
    rows = cotangent.shape[1]
    lists = jnp.transpose(block_ids, (0, 2, 1))
    sent = pl.pallas_call(
        forward_kernel,
        out_shape=jax.ShapeDtypeStruct((peers, 8, side), BF16),
        in_specs=[HBM] * 5,
        out_specs=VMEM,
        scratch_shapes=[
            pltpu.VMEM(adjacency.shape[1:], BF16),
            pltpu.SMEM(lists.shape, jnp.int32),
            pltpu.SMEM(block_counts.shape, jnp.int32),
            pltpu.VMEM(node_ids.shape, jnp.int32),
            pltpu.VMEM(feature_table.shape, BF16),
            pltpu.VMEM((feature_table.shape[1] // LOW * chans, LOW), F32),
            pltpu.VMEM((sources, 8, side), F32),
            pltpu.VMEM((peers, 8, side), F32),
            pltpu.SemaphoreType.DMA((ADJ_PARTS + 4,)),
        ],
        compiler_params=params(24),
        name="forward",
    )(*[in_hbm(v) for v in (lists, block_counts, node_ids, feature_table, adjacency)])
    arrived = lax.all_to_all(sent, "feat", split_axis=0, concat_axis=0, tiled=True)
    hid_vmem, send = pl.pallas_call(
        dense_kernel,
        out_shape=(
            jax.ShapeDtypeStruct(cotangent.shape, BF16),
            jax.ShapeDtypeStruct((peers, chans, 7 * side), BF16),
        ),
        in_specs=[VMEM] * 5,
        out_specs=(VMEM, VMEM),
        compiler_params=params(16),
        name="dense",
    )(arrived, self_weight, neigh_weight, bias_vector.reshape(1, hid), cotangent)
    got = lax.all_to_all(send, "feat", split_axis=0, concat_axis=0, tiled=True)
    partial = pl.pallas_call(
        feat_sum_kernel,
        out_shape=jax.ShapeDtypeStruct((reps, chans, 5 * side), BF16),
        in_specs=[VMEM],
        out_specs=VMEM,
        compiler_params=params(8),
        name="feat_sum",
    )(got)
    over_rep = lax.all_to_all(partial, "rep", split_axis=0, concat_axis=0, tiled=True)
    factor = float(rows * peers * reps) ** (-0.5)
    pieces, bias_grad = pl.pallas_call(
        lambda *refs: rep_sum_kernel(factor, *refs),
        out_shape=(
            jax.ShapeDtypeStruct((peers, chans, 4 * side), BF16),
            jax.ShapeDtypeStruct((1, hid), F32),
        ),
        in_specs=[VMEM],
        out_specs=(VMEM, VMEM),
        compiler_params=params(8),
        name="rep_sum",
    )(over_rep)
    whole = lax.all_to_all(pieces, "feat", split_axis=0, concat_axis=0, tiled=True)
    feature_grad, hidden = pl.pallas_call(
        backward_kernel,
        out_shape=(
            jax.ShapeDtypeStruct((1, chans, node_count), BF16),
            jax.ShapeDtypeStruct(cotangent.shape, BF16),
        ),
        in_specs=[SMEM, SMEM, VMEM, VMEM, HBM],
        out_specs=(VMEM, VMEM),
        scratch_shapes=[
            pltpu.VMEM(adjacency.shape[1:], BF16),
            pltpu.VMEM((sources + 1, chans, side), F32),
            pltpu.SemaphoreType.DMA((ADJ_PARTS,)),
        ],
        compiler_params=params(24),
        cost_estimate=pl.CostEstimate(
            flops=2 * 16 * adjacency.size, bytes_accessed=2 * adjacency.size, transcendentals=0
        ),
        name="spread_back",
    )(lists, block_counts, got, hid_vmem, in_hbm(adjacency))
    self_grad, neigh_grad = pl.pallas_call(
        assemble_kernel,
        out_shape=(
            jax.ShapeDtypeStruct((feats, hid), F32),
            jax.ShapeDtypeStruct((feats, hid), F32),
        ),
        in_specs=[VMEM],
        out_specs=(VMEM, VMEM),
        compiler_params=params(8),
        name="assemble",
    )(whole)
    return hidden, feature_grad, self_grad, neigh_grad, bias_grad.reshape(hid)


def solution(mesh):
    return jax.shard_map(
        local,
        mesh=mesh,
        in_specs=(
            P("feat", None),
            P("rep", None),
            P("rep", None, None),
            P("rep", None),
            P("rep", None, None, None, None),
            P(),
            P(),
            P(),
            P("rep", "feat", None),
        ),
        out_specs=(P("rep", "feat", None), P("rep", "feat", None), P(), P(), P()),
        check_vma=False,
    )
```

```python
import jax
import jax.numpy as jnp
from jax import lax
from jax.experimental import pallas as pl
from jax.experimental.pallas import tpu as pltpu
from jax.sharding import PartitionSpec as P

F32 = jnp.float32
BF16 = jnp.bfloat16
HELD = 16
LOW = 256
CHUNK = 512


def forward_kernel(
    lists_hbm,
    counts_hbm,
    nodes_hbm,
    table_hbm,
    adj_hbm,
    out_ref,
    held,
    rest,
    ids_ref,
    counts_ref,
    nodes_ref,
    table_ref,
    rows_f32,
    feats,
    staged,
    sems,
):
    blocks, _, side, _ = adj_hbm.shape[1:]
    copies = [
        pltpu.make_async_copy(adj_hbm.at[0, pl.ds(0, HELD)], held, sems.at[0]),
        pltpu.make_async_copy(adj_hbm.at[0, pl.ds(HELD, blocks - HELD)], rest, sems.at[1]),
    ]
    inputs = [
        pltpu.make_async_copy(table_hbm, table_ref, sems.at[2]),
        pltpu.make_async_copy(nodes_hbm, nodes_ref, sems.at[3]),
    ]
    lists = [
        pltpu.make_async_copy(lists_hbm, ids_ref, sems.at[4]),
        pltpu.make_async_copy(counts_hbm, counts_ref, sems.at[5]),
    ]
    for copy in inputs + lists + copies:
        copy.start()
    for copy in inputs:
        copy.wait()
    chans = table_ref.shape[0]
    groups = table_ref.shape[1] // LOW
    for q in range(groups):
        rows_f32[q * chans : (q + 1) * chans, :] = table_ref[:, q * LOW : (q + 1) * LOW].astype(F32)
    table_rows = rows_f32[...].astype(BF16)
    node_count = nodes_ref.shape[1]
    column = lax.broadcasted_iota(jnp.int32, (LOW, CHUNK), 0).astype(F32).astype(BF16)
    one = jnp.ones((LOW, CHUNK), BF16)
    zero = jnp.zeros((LOW, CHUNK), BF16)
    for start in range(0, node_count, CHUNK):
        ids = nodes_ref[:, start : start + CHUNK]
        low = ids & (LOW - 1)
        high = ids // LOW
        onehot = jnp.where(column == low.astype(F32).astype(BF16), one, zero)
        spread = jnp.dot(table_rows, onehot, preferred_element_type=F32)
        group = lax.broadcasted_iota(jnp.int32, spread.shape, 0) // chans
        kept = jnp.where(group == high, spread, 0.0)
        two = jnp.sum(kept.reshape(-1, 8, CHUNK), axis=0)
        both = two + pltpu.roll(two, 4, 0)
        for j in range(CHUNK // 128):
            feats[start // 128 + j] = both[:, j * 128 : (j + 1) * 128]
    for copy in lists:
        copy.wait()
    depth = ids_ref.shape[1]
    upper = lax.broadcasted_iota(jnp.int32, (8, side), 0) < chans
    for b in range(blocks):
        if b in (0, HELD):
            copies[b // HELD].wait()
        adj = held[b] if b < HELD else rest[b - HELD]
        count = counts_ref[0, b]
        picked = [
            jnp.where(k < count, feats[ids_ref[0, k, b]], 0.0) for k in range(depth)
        ]
        lhs = jnp.concatenate(picked, axis=1).astype(BF16)
        agg = jnp.dot(lhs, adj.reshape(depth * side, side), preferred_element_type=F32)
        staged[b] = jnp.where(upper, feats[b], agg)
    out_ref[...] = staged[...].astype(BF16)


def dense_kernel(x_ref, sw_ref, nw_ref, bias_ref, cot_ref, hidden_ref, send_ref):
    feats = sw_ref.shape[0]
    hid = sw_ref.shape[1]
    sw = sw_ref[...].astype(F32).reshape(feats // 8, 8, hid)
    nw = nw_ref[...].astype(F32).reshape(feats // 8, 8, hid)
    upper = lax.broadcasted_iota(jnp.int32, sw.shape, 1) < 4
    even = jnp.where(upper, sw, pltpu.roll(nw, 4, 1))
    odd = jnp.where(upper, pltpu.roll(sw, 4, 1), nw)
    weight = jnp.concatenate([even, odd], axis=1).reshape(2 * feats, hid).astype(BF16)
    rows = x_ref.shape[2]
    x = x_ref[...].reshape(2 * feats, rows)
    preact = lax.dot_general(x, weight, (((0,), (0,)), ((), ())), preferred_element_type=F32)
    preact = preact + bias_ref[...]
    sig = jax.nn.sigmoid(preact)
    hidden_ref[0] = (preact * sig).astype(BF16)
    grad_pre = (cot_ref[0].astype(F32) * sig * (1.0 + preact * (1.0 - sig))).astype(BF16)
    grads = jnp.dot(x, grad_pre, preferred_element_type=F32)
    back = lax.dot_general(
        weight, grad_pre, (((1,), (1,)), ((), ())), preferred_element_type=F32
    )
    bias_sum = jnp.sum(grad_pre.astype(F32), axis=0, keepdims=True)
    half = hid // 2
    tail = split_rows(bias_sum[:, :half], bias_sum[:, half:])
    peers = send_ref.shape[0]
    values = [back.reshape(peers, 8, rows)]
    values += [grads[:, at : at + half].reshape(peers, 8, half) for at in (0, half)]
    parts = [v[:, at : at + 4] for v in values for at in (0, 4)]
    parts.append(jnp.broadcast_to(tail[None], (peers, 4, half)))
    send_ref[...] = jnp.concatenate(parts, axis=2).astype(BF16)


def split_rows(first, second):
    place = lax.broadcasted_iota(jnp.int32, (4, first.shape[1]), 0)
    first_hi = first.astype(BF16).astype(F32)
    second_hi = second.astype(BF16).astype(F32)
    out = jnp.where(place == 0, first_hi, 0.0)
    out = jnp.where(place == 1, second_hi, out)
    out = jnp.where(place == 2, first - first_hi, out)
    return jnp.where(place == 3, second - second_hi, out)


def add_up(parts):
    total = jnp.sum(parts, axis=0)
    cols = total.shape[1] - 128
    low = total[:, cols:]
    return total[:, :cols], low[0:1] + low[2:3], low[1:2] + low[3:4]


def feat_sum_kernel(got_ref, out_ref):
    total, first, second = add_up(got_ref[...].astype(F32)[:, :, 256:])
    whole = jnp.concatenate([total, split_rows(first, second)], axis=1).astype(BF16)
    out_ref[...] = jnp.broadcast_to(whole[None], out_ref.shape)


def rep_sum_kernel(factor, got_ref, after_ref, out_ref, bias_ref):
    total, first, second = add_up(got_ref[...].astype(F32))
    bias_ref[...] = factor * jnp.concatenate([first, second], axis=1)
    out_ref[...] = jnp.broadcast_to((factor * total).astype(BF16)[None], out_ref.shape)


def assemble_kernel(
    got_ref, bias_ref, self_hbm, neigh_hbm, bias_hbm, self_ref, neigh_ref, sems
):
    side = got_ref.shape[2] // 4
    copies = [pltpu.make_async_copy(bias_ref, bias_hbm, sems.at[2])]
    copies[0].start()
    for j, (out_ref, out_hbm) in enumerate(((self_ref, self_hbm), (neigh_ref, neigh_hbm))):
        for h in range(2):
            at = (2 * h + j) * side
            got = got_ref[:, :, at : at + side].astype(F32)
            out_ref[:, h * side : (h + 1) * side] = got.reshape(-1, side)
        copy = pltpu.make_async_copy(out_ref, out_hbm, sems.at[j])
        copy.start()
        copies.append(copy)
    for copy in copies:
        copy.wait()


def backward_kernel(
    ids_ref, counts_ref, got_ref, hid_ref, held, adj_hbm, out_ref, hidden_ref, rest, acc, sems
):
    blocks, _, side, _ = adj_hbm.shape[1:]
    copy = pltpu.make_async_copy(
        adj_hbm.at[0, pl.ds(HELD, blocks - HELD)], rest, sems.at[0]
    )
    copy.start()
    hidden_ref[...] = hid_ref[...]
    acc[...] = jnp.zeros_like(acc)
    depth = ids_ref.shape[1]
    sources = acc.shape[0] - 1
    for b in range(blocks):
        if b == HELD:
            copy.wait()
        adj = held[b] if b < HELD else rest[b - HELD]
        count = counts_ref[0, b]
        lhs = got_ref[b, :, side : 2 * side]
        contrib = lax.dot_general(
            lhs,
            adj.reshape(depth * side, side),
            (((1,), (1,)), ((), ())),
            preferred_element_type=F32,
        )
        for k in range(depth):
            place = jnp.where(k < count, ids_ref[0, k, b], sources)
            acc[place] = acc[place] + contrib[:, k * side : (k + 1) * side]
    for n in range(sources):
        total = acc[n]
        if n < blocks:
            total = total + got_ref[n, :, 0:side].astype(F32)
        out_ref[0, :, n * side : (n + 1) * side] = total.astype(BF16)


SMEM = pl.BlockSpec(memory_space=pltpu.SMEM)
VMEM = pl.BlockSpec(memory_space=pltpu.VMEM)
HBM = pl.BlockSpec(memory_space=pl.ANY)


def in_hbm(array):
    return pltpu.with_memory_space_constraint(array, pltpu.HBM)


def params(mib):
    return pltpu.CompilerParams(vmem_limit_bytes=mib * 1024 * 1024)


def local(
    feature_table,
    node_ids,
    block_ids,
    block_counts,
    adjacency,
    self_weight,
    neigh_weight,
    bias_vector,
    cotangent,
):
    chans = feature_table.shape[0]
    node_count = node_ids.shape[1]
    blocks, depth, side = adjacency.shape[1:4]
    sources = node_count // side
    peers = lax.axis_size("feat")
    reps = lax.axis_size("rep")
    feats, hid = self_weight.shape
    rows = cotangent.shape[1]
    lists = jnp.transpose(block_ids, (0, 2, 1))
    held_shape = (HELD, depth, side, side)
    rest_shape = (blocks - HELD, depth, side, side)
    sent, held = pl.pallas_call(
        forward_kernel,
        out_shape=(
            jax.ShapeDtypeStruct((peers, 8, side), BF16),
            jax.ShapeDtypeStruct(held_shape, BF16),
        ),
        in_specs=[HBM] * 5,
        out_specs=(VMEM, VMEM),
        scratch_shapes=[
            pltpu.VMEM(rest_shape, BF16),
            pltpu.SMEM(lists.shape, jnp.int32),
            pltpu.SMEM(block_counts.shape, jnp.int32),
            pltpu.VMEM(node_ids.shape, jnp.int32),
            pltpu.VMEM(feature_table.shape, BF16),
            pltpu.VMEM((feature_table.shape[1] // LOW * chans, LOW), F32),
            pltpu.VMEM((sources, 8, side), F32),
            pltpu.VMEM((peers, 8, side), F32),
            pltpu.SemaphoreType.DMA((6,)),
        ],
        compiler_params=params(24),
        name="forward",
    )(*[in_hbm(v) for v in (lists, block_counts, node_ids, feature_table, adjacency)])
    arrived = lax.all_to_all(sent, "feat", split_axis=0, concat_axis=0, tiled=True)
    hid_vmem, send = pl.pallas_call(
        dense_kernel,
        out_shape=(
            jax.ShapeDtypeStruct(cotangent.shape, BF16),
            jax.ShapeDtypeStruct((peers, chans, 7 * side), BF16),
        ),
        in_specs=[VMEM] * 5,
        out_specs=(VMEM, VMEM),
        compiler_params=params(16),
        name="dense",
    )(arrived, self_weight, neigh_weight, bias_vector.reshape(1, hid), cotangent)
    got = lax.all_to_all(send, "feat", split_axis=0, concat_axis=0, tiled=True)
    partial = pl.pallas_call(
        feat_sum_kernel,
        out_shape=jax.ShapeDtypeStruct((reps, chans, 5 * side), BF16),
        in_specs=[VMEM],
        out_specs=VMEM,
        compiler_params=params(8),
        name="feat_sum",
    )(got)
    over_rep = lax.all_to_all(partial, "rep", split_axis=0, concat_axis=0, tiled=True)
    factor = float(rows * peers * reps) ** (-0.5)
    feature_grad, hidden = pl.pallas_call(
        backward_kernel,
        out_shape=(
            jax.ShapeDtypeStruct((1, chans, node_count), BF16),
            jax.ShapeDtypeStruct(cotangent.shape, BF16),
        ),
        in_specs=[SMEM, SMEM, VMEM, VMEM, VMEM, HBM],
        out_specs=(VMEM, VMEM),
        scratch_shapes=[
            pltpu.VMEM(rest_shape, BF16),
            pltpu.VMEM((sources + 1, chans, side), F32),
            pltpu.SemaphoreType.DMA((1,)),
        ],
        compiler_params=params(24),
        cost_estimate=pl.CostEstimate(
            flops=2 * 16 * adjacency.size, bytes_accessed=2 * adjacency.size, transcendentals=0
        ),
        name="spread_back",
    )(lists, block_counts, got, hid_vmem, held, in_hbm(adjacency))
    pieces, bias_sum = pl.pallas_call(
        lambda *refs: rep_sum_kernel(factor, *refs),
        out_shape=(
            jax.ShapeDtypeStruct((peers, chans, 4 * side), BF16),
            jax.ShapeDtypeStruct((1, hid), F32),
        ),
        in_specs=[VMEM, HBM],
        out_specs=(VMEM, VMEM),
        compiler_params=params(8),
        name="rep_sum",
    )(over_rep, in_hbm(hidden))
    whole = lax.all_to_all(pieces, "feat", split_axis=0, concat_axis=0, tiled=True)
    self_grad, neigh_grad, bias_grad = pl.pallas_call(
        assemble_kernel,
        out_shape=(
            jax.ShapeDtypeStruct((feats, hid), F32),
            jax.ShapeDtypeStruct((feats, hid), F32),
            jax.ShapeDtypeStruct((1, hid), F32),
        ),
        in_specs=[VMEM, VMEM],
        out_specs=(HBM, HBM, HBM),
        scratch_shapes=[
            pltpu.VMEM((feats, hid), F32),
            pltpu.VMEM((feats, hid), F32),
            pltpu.SemaphoreType.DMA((3,)),
        ],
        compiler_params=params(8),
        name="assemble",
    )(whole, bias_sum)
    return hidden, feature_grad, self_grad, neigh_grad, bias_grad.reshape(hid)


def solution(mesh):
    return jax.shard_map(
        local,
        mesh=mesh,
        in_specs=(
            P("feat", None),
            P("rep", None),
            P("rep", None, None),
            P("rep", None),
            P("rep", None, None, None, None),
            P(),
            P(),
            P(),
            P("rep", "feat", None),
        ),
        out_specs=(P("rep", "feat", None), P("rep", "feat", None), P(), P(), P()),
        check_vma=False,
    )
```

```python
import jax
import jax.numpy as jnp
from jax import lax
from jax.experimental import pallas as pl
from jax.experimental.pallas import tpu as pltpu
from jax.sharding import PartitionSpec as P

F32 = jnp.float32
BF16 = jnp.bfloat16
HELD = 16
LOW = 256
CHUNK = 512


def forward_kernel(
    lists_hbm,
    counts_hbm,
    nodes_hbm,
    table_hbm,
    adj_hbm,
    out_ref,
    held,
    rest,
    ids_ref,
    counts_ref,
    nodes_ref,
    table_ref,
    rows_f32,
    feats,
    staged,
    sems,
):
    blocks, _, side, _ = adj_hbm.shape[1:]
    copies = [
        pltpu.make_async_copy(adj_hbm.at[0, pl.ds(0, HELD)], held, sems.at[0]),
        pltpu.make_async_copy(adj_hbm.at[0, pl.ds(HELD, blocks - HELD)], rest, sems.at[1]),
    ]
    inputs = [
        pltpu.make_async_copy(table_hbm, table_ref, sems.at[2]),
        pltpu.make_async_copy(nodes_hbm, nodes_ref, sems.at[3]),
    ]
    lists = [
        pltpu.make_async_copy(lists_hbm, ids_ref, sems.at[4]),
        pltpu.make_async_copy(counts_hbm, counts_ref, sems.at[5]),
    ]
    for copy in inputs + lists + copies:
        copy.start()
    for copy in inputs:
        copy.wait()
    chans = table_ref.shape[0]
    groups = table_ref.shape[1] // LOW
    for q in range(groups):
        rows_f32[q * chans : (q + 1) * chans, :] = table_ref[:, q * LOW : (q + 1) * LOW].astype(F32)
    table_rows = rows_f32[...].astype(BF16)
    node_count = nodes_ref.shape[1]
    column = lax.broadcasted_iota(jnp.int32, (LOW, CHUNK), 0).astype(F32).astype(BF16)
    one = jnp.ones((LOW, CHUNK), BF16)
    zero = jnp.zeros((LOW, CHUNK), BF16)
    for start in range(0, node_count, CHUNK):
        ids = nodes_ref[:, start : start + CHUNK]
        low = ids & (LOW - 1)
        high = ids // LOW
        onehot = jnp.where(column == low.astype(F32).astype(BF16), one, zero)
        spread = jnp.dot(table_rows, onehot, preferred_element_type=F32)
        group = lax.broadcasted_iota(jnp.int32, spread.shape, 0) // chans
        kept = jnp.where(group == high, spread, 0.0)
        two = jnp.sum(kept.reshape(-1, 8, CHUNK), axis=0)
        both = two + pltpu.roll(two, 4, 0)
        for j in range(CHUNK // 128):
            feats[start // 128 + j] = both[:, j * 128 : (j + 1) * 128]
    for copy in lists:
        copy.wait()
    depth = ids_ref.shape[1]
    upper = lax.broadcasted_iota(jnp.int32, (8, side), 0) < chans
    for b in range(blocks):
        if b in (0, HELD):
            copies[b // HELD].wait()
        adj = held[b] if b < HELD else rest[b - HELD]
        count = counts_ref[0, b]
        picked = [
            jnp.where(k < count, feats[ids_ref[0, k, b]], 0.0) for k in range(depth)
        ]
        lhs = jnp.concatenate(picked, axis=1).astype(BF16)
        agg = jnp.dot(lhs, adj.reshape(depth * side, side), preferred_element_type=F32)
        staged[b] = jnp.where(upper, feats[b], agg)
    out_ref[...] = staged[...].astype(BF16)


def dense_kernel(x_ref, sw_ref, nw_ref, bias_ref, cot_ref, hidden_ref, send_ref):
    feats = sw_ref.shape[0]
    hid = sw_ref.shape[1]
    sw = sw_ref[...].astype(F32).reshape(feats // 8, 8, hid)
    nw = nw_ref[...].astype(F32).reshape(feats // 8, 8, hid)
    upper = lax.broadcasted_iota(jnp.int32, sw.shape, 1) < 4
    even = jnp.where(upper, sw, pltpu.roll(nw, 4, 1))
    odd = jnp.where(upper, pltpu.roll(sw, 4, 1), nw)
    weight = jnp.concatenate([even, odd], axis=1).reshape(2 * feats, hid).astype(BF16)
    rows = x_ref.shape[2]
    x = x_ref[...].reshape(2 * feats, rows)
    preact = lax.dot_general(x, weight, (((0,), (0,)), ((), ())), preferred_element_type=F32)
    preact = preact + bias_ref[...]
    sig = jax.nn.sigmoid(preact)
    hidden_ref[0] = (preact * sig).astype(BF16)
    grad_pre = (cot_ref[0].astype(F32) * sig * (1.0 + preact * (1.0 - sig))).astype(BF16)
    grads = jnp.dot(x, grad_pre, preferred_element_type=F32)
    back = lax.dot_general(
        weight, grad_pre, (((1,), (1,)), ((), ())), preferred_element_type=F32
    )
    bias_sum = jnp.sum(grad_pre.astype(F32), axis=0, keepdims=True)
    half = hid // 2
    peers = send_ref.shape[0]
    values = [back.reshape(peers, 8, rows)]
    values += [grads[:, at : at + half].reshape(peers, 8, half) for at in (0, half)]
    parts = [v[:, at : at + 2] for v in values for at in (0, 2, 4, 6)]
    tail = jnp.concatenate([bias_sum[:, :half], bias_sum[:, half:]], axis=0)
    parts.append(jnp.broadcast_to(tail[None], (peers, 2, half)))
    send_ref[...] = jnp.concatenate(parts, axis=2).astype(BF16)


def feat_sum_kernel(got_ref, out_ref):
    total = jnp.sum(got_ref[...].astype(F32)[:, :, 512:], axis=0)
    out_ref[...] = jnp.broadcast_to(total.astype(BF16)[None], out_ref.shape)


def two_rows(value, at):
    return jnp.concatenate([value[:, at : at + 128], value[:, at + 128 : at + 256]], axis=0)


def rep_sum_kernel(factor, got_ref, after_ref, out_ref, bias_ref):
    total = factor * jnp.sum(got_ref[...].astype(F32), axis=0)
    bias_ref[...] = jnp.concatenate([total[0:1, 1024:], total[1:2, 1024:]], axis=1)
    whole = jnp.concatenate([two_rows(total, at) for at in (0, 256, 512, 768)], axis=1)
    out_ref[...] = jnp.broadcast_to(whole.astype(BF16)[None], out_ref.shape)


def assemble_kernel(
    got_ref, bias_ref, self_hbm, neigh_hbm, bias_hbm, self_ref, neigh_ref, sems
):
    side = got_ref.shape[2] // 4
    copies = [pltpu.make_async_copy(bias_ref, bias_hbm, sems.at[2])]
    copies[0].start()
    for j, (out_ref, out_hbm) in enumerate(((self_ref, self_hbm), (neigh_ref, neigh_hbm))):
        for h in range(2):
            at = (2 * h + j) * side
            got = got_ref[:, :, at : at + side].astype(F32)
            out_ref[:, h * side : (h + 1) * side] = got.reshape(-1, side)
        copy = pltpu.make_async_copy(out_ref, out_hbm, sems.at[j])
        copy.start()
        copies.append(copy)
    for copy in copies:
        copy.wait()


def backward_kernel(
    ids_ref, counts_ref, got_ref, hid_ref, held, adj_hbm, out_ref, hidden_ref, rest, acc, sems
):
    blocks, _, side, _ = adj_hbm.shape[1:]
    copy = pltpu.make_async_copy(
        adj_hbm.at[0, pl.ds(HELD, blocks - HELD)], rest, sems.at[0]
    )
    copy.start()
    hidden_ref[...] = hid_ref[...]
    acc[...] = jnp.zeros_like(acc)
    depth = ids_ref.shape[1]
    sources = acc.shape[0] - 1
    for b in range(blocks):
        if b == HELD:
            copy.wait()
        adj = held[b] if b < HELD else rest[b - HELD]
        count = counts_ref[0, b]
        lhs = two_rows(got_ref[b].astype(F32), 2 * side).astype(BF16)
        contrib = lax.dot_general(
            lhs,
            adj.reshape(depth * side, side),
            (((1,), (1,)), ((), ())),
            preferred_element_type=F32,
        )
        for k in range(depth):
            place = jnp.where(k < count, ids_ref[0, k, b], sources)
            acc[place] = acc[place] + contrib[:, k * side : (k + 1) * side]
    for n in range(sources):
        total = acc[n]
        if n < blocks:
            total = total + two_rows(got_ref[n].astype(F32), 0)
        out_ref[0, :, n * side : (n + 1) * side] = total.astype(BF16)


SMEM = pl.BlockSpec(memory_space=pltpu.SMEM)
VMEM = pl.BlockSpec(memory_space=pltpu.VMEM)
HBM = pl.BlockSpec(memory_space=pl.ANY)


def in_hbm(array):
    return pltpu.with_memory_space_constraint(array, pltpu.HBM)


def params(mib):
    return pltpu.CompilerParams(vmem_limit_bytes=mib * 1024 * 1024)


def local(
    feature_table,
    node_ids,
    block_ids,
    block_counts,
    adjacency,
    self_weight,
    neigh_weight,
    bias_vector,
    cotangent,
):
    chans = feature_table.shape[0]
    node_count = node_ids.shape[1]
    blocks, depth, side = adjacency.shape[1:4]
    sources = node_count // side
    peers = lax.axis_size("feat")
    reps = lax.axis_size("rep")
    feats, hid = self_weight.shape
    rows = cotangent.shape[1]
    lists = jnp.transpose(block_ids, (0, 2, 1))
    held_shape = (HELD, depth, side, side)
    rest_shape = (blocks - HELD, depth, side, side)
    sent, held = pl.pallas_call(
        forward_kernel,
        out_shape=(
            jax.ShapeDtypeStruct((peers, 8, side), BF16),
            jax.ShapeDtypeStruct(held_shape, BF16),
        ),
        in_specs=[HBM] * 5,
        out_specs=(VMEM, VMEM),
        scratch_shapes=[
            pltpu.VMEM(rest_shape, BF16),
            pltpu.SMEM(lists.shape, jnp.int32),
            pltpu.SMEM(block_counts.shape, jnp.int32),
            pltpu.VMEM(node_ids.shape, jnp.int32),
            pltpu.VMEM(feature_table.shape, BF16),
            pltpu.VMEM((feature_table.shape[1] // LOW * chans, LOW), F32),
            pltpu.VMEM((sources, 8, side), F32),
            pltpu.VMEM((peers, 8, side), F32),
            pltpu.SemaphoreType.DMA((6,)),
        ],
        compiler_params=params(24),
        name="forward",
    )(*[in_hbm(v) for v in (lists, block_counts, node_ids, feature_table, adjacency)])
    arrived = lax.all_to_all(sent, "feat", split_axis=0, concat_axis=0, tiled=True)
    hid_vmem, send = pl.pallas_call(
        dense_kernel,
        out_shape=(
            jax.ShapeDtypeStruct(cotangent.shape, BF16),
            jax.ShapeDtypeStruct((peers, 2, 13 * side), BF16),
        ),
        in_specs=[VMEM] * 5,
        out_specs=(VMEM, VMEM),
        compiler_params=params(16),
        name="dense",
    )(arrived, self_weight, neigh_weight, bias_vector.reshape(1, hid), cotangent)
    got = lax.all_to_all(send, "feat", split_axis=0, concat_axis=0, tiled=True)
    partial = pl.pallas_call(
        feat_sum_kernel,
        out_shape=jax.ShapeDtypeStruct((reps, 2, 9 * side), BF16),
        in_specs=[VMEM],
        out_specs=VMEM,
        compiler_params=params(8),
        name="feat_sum",
    )(got)
    order = [2 * ((3 * y) % (reps // 2)) + core for y in range(reps // 2) for core in range(2)]
    over_rep = lax.all_to_all(
        partial, "rep", split_axis=0, concat_axis=0, tiled=True, axis_index_groups=[order]
    )
    factor = float(rows * peers * reps) ** (-0.5)
    feature_grad, hidden = pl.pallas_call(
        backward_kernel,
        out_shape=(
            jax.ShapeDtypeStruct((1, chans, node_count), BF16),
            jax.ShapeDtypeStruct(cotangent.shape, BF16),
        ),
        in_specs=[SMEM, SMEM, VMEM, VMEM, VMEM, HBM],
        out_specs=(VMEM, VMEM),
        scratch_shapes=[
            pltpu.VMEM(rest_shape, BF16),
            pltpu.VMEM((sources + 1, chans, side), F32),
            pltpu.SemaphoreType.DMA((1,)),
        ],
        compiler_params=params(24),
        cost_estimate=pl.CostEstimate(
            flops=2 * 16 * adjacency.size, bytes_accessed=2 * adjacency.size, transcendentals=0
        ),
        name="spread_back",
    )(lists, block_counts, got, hid_vmem, held, in_hbm(adjacency))
    pieces, bias_sum = pl.pallas_call(
        lambda *refs: rep_sum_kernel(factor, *refs),
        out_shape=(
            jax.ShapeDtypeStruct((peers, chans, 4 * side), BF16),
            jax.ShapeDtypeStruct((1, hid), F32),
        ),
        in_specs=[VMEM, HBM],
        out_specs=(VMEM, VMEM),
        compiler_params=params(8),
        name="rep_sum",
    )(over_rep, in_hbm(hidden))
    whole = lax.all_to_all(pieces, "feat", split_axis=0, concat_axis=0, tiled=True)
    self_grad, neigh_grad, bias_grad = pl.pallas_call(
        assemble_kernel,
        out_shape=(
            jax.ShapeDtypeStruct((feats, hid), F32),
            jax.ShapeDtypeStruct((feats, hid), F32),
            jax.ShapeDtypeStruct((1, hid), F32),
        ),
        in_specs=[VMEM, VMEM],
        out_specs=(HBM, HBM, HBM),
        scratch_shapes=[
            pltpu.VMEM((feats, hid), F32),
            pltpu.VMEM((feats, hid), F32),
            pltpu.SemaphoreType.DMA((3,)),
        ],
        compiler_params=params(8),
        name="assemble",
    )(whole, bias_sum)
    return hidden, feature_grad, self_grad, neigh_grad, bias_grad.reshape(hid)


def solution(mesh):
    return jax.shard_map(
        local,
        mesh=mesh,
        in_specs=(
            P("feat", None),
            P("rep", None),
            P("rep", None, None),
            P("rep", None),
            P("rep", None, None, None, None),
            P(),
            P(),
            P(),
            P("rep", "feat", None),
        ),
        out_specs=(P("rep", "feat", None), P("rep", "feat", None), P(), P(), P()),
        check_vma=False,
    )
```

```python
import jax
import jax.numpy as jnp
from jax import lax
from jax.experimental import pallas as pl
from jax.experimental.pallas import tpu as pltpu
from jax.sharding import PartitionSpec as P

F32 = jnp.float32
BF16 = jnp.bfloat16
HELD = 16
FEAT_ORDER = [4 * ((3 * z) % 8) + x for z in range(8) for x in range(4)]
LOW = 256
CHUNK = 512


def forward_kernel(
    lists_hbm,
    counts_hbm,
    nodes_hbm,
    table_hbm,
    adj_hbm,
    out_ref,
    held,
    rest,
    ids_ref,
    counts_ref,
    nodes_ref,
    table_ref,
    rows_f32,
    feats,
    staged,
    sems,
):
    blocks, _, side, _ = adj_hbm.shape[1:]
    copies = [
        pltpu.make_async_copy(adj_hbm.at[0, pl.ds(0, HELD)], held, sems.at[0]),
        pltpu.make_async_copy(adj_hbm.at[0, pl.ds(HELD, blocks - HELD)], rest, sems.at[1]),
    ]
    inputs = [
        pltpu.make_async_copy(table_hbm, table_ref, sems.at[2]),
        pltpu.make_async_copy(nodes_hbm, nodes_ref, sems.at[3]),
    ]
    lists = [
        pltpu.make_async_copy(lists_hbm, ids_ref, sems.at[4]),
        pltpu.make_async_copy(counts_hbm, counts_ref, sems.at[5]),
    ]
    for copy in inputs + lists + copies:
        copy.start()
    for copy in inputs:
        copy.wait()
    chans = table_ref.shape[0]
    groups = table_ref.shape[1] // LOW
    for q in range(groups):
        rows_f32[q * chans : (q + 1) * chans, :] = table_ref[:, q * LOW : (q + 1) * LOW].astype(F32)
    table_rows = rows_f32[...].astype(BF16)
    node_count = nodes_ref.shape[1]
    column = lax.broadcasted_iota(jnp.int32, (LOW, CHUNK), 0).astype(F32).astype(BF16)
    one = jnp.ones((LOW, CHUNK), BF16)
    zero = jnp.zeros((LOW, CHUNK), BF16)
    for start in range(0, node_count, CHUNK):
        ids = nodes_ref[:, start : start + CHUNK]
        low = ids & (LOW - 1)
        high = ids // LOW
        onehot = jnp.where(column == low.astype(F32).astype(BF16), one, zero)
        spread = jnp.dot(table_rows, onehot, preferred_element_type=F32)
        group = lax.broadcasted_iota(jnp.int32, spread.shape, 0) // chans
        kept = jnp.where(group == high, spread, 0.0)
        two = jnp.sum(kept.reshape(-1, 8, CHUNK), axis=0)
        both = two + pltpu.roll(two, 4, 0)
        for j in range(CHUNK // 128):
            feats[start // 128 + j] = both[:, j * 128 : (j + 1) * 128]
    for copy in lists:
        copy.wait()
    depth = ids_ref.shape[1]
    upper = lax.broadcasted_iota(jnp.int32, (8, side), 0) < chans
    for b in range(blocks):
        if b in (0, HELD):
            copies[b // HELD].wait()
        adj = held[b] if b < HELD else rest[b - HELD]
        count = counts_ref[0, b]
        picked = [
            jnp.where(k < count, feats[ids_ref[0, k, b]], 0.0) for k in range(depth)
        ]
        lhs = jnp.concatenate(picked, axis=1).astype(BF16)
        agg = jnp.dot(lhs, adj.reshape(depth * side, side), preferred_element_type=F32)
        staged[FEAT_ORDER.index(b)] = jnp.where(upper, feats[b], agg)
    out_ref[...] = staged[...].astype(BF16)


def dense_kernel(x_ref, sw_ref, nw_ref, bias_ref, cot_ref, hidden_ref, send_ref):
    feats = sw_ref.shape[0]
    hid = sw_ref.shape[1]
    sw = sw_ref[...].astype(F32).reshape(feats // 8, 8, hid)
    nw = nw_ref[...].astype(F32).reshape(feats // 8, 8, hid)
    upper = lax.broadcasted_iota(jnp.int32, sw.shape, 1) < 4
    even = jnp.where(upper, sw, pltpu.roll(nw, 4, 1))
    odd = jnp.where(upper, pltpu.roll(sw, 4, 1), nw)
    weight = jnp.concatenate([even, odd], axis=1).reshape(feats // 4, 8, hid)
    weight = jnp.concatenate([weight[i : i + 1] for i in FEAT_ORDER], axis=0)
    weight = weight.reshape(2 * feats, hid).astype(BF16)
    rows = x_ref.shape[2]
    x = x_ref[...].reshape(2 * feats, rows)
    preact = lax.dot_general(x, weight, (((0,), (0,)), ((), ())), preferred_element_type=F32)
    preact = preact + bias_ref[...]
    sig = jax.nn.sigmoid(preact)
    hidden_ref[0] = (preact * sig).astype(BF16)
    grad_pre = (cot_ref[0].astype(F32) * sig * (1.0 + preact * (1.0 - sig))).astype(BF16)
    grads = jnp.dot(x, grad_pre, preferred_element_type=F32)
    back = lax.dot_general(
        weight, grad_pre, (((1,), (1,)), ((), ())), preferred_element_type=F32
    )
    bias_sum = jnp.sum(grad_pre.astype(F32), axis=0, keepdims=True)
    half = hid // 2
    peers = send_ref.shape[0]
    values = [back.reshape(peers, 8, rows)]
    values += [grads[:, at : at + half].reshape(peers, 8, half) for at in (0, half)]
    parts = [v[:, at : at + 2] for v in values for at in (0, 2, 4, 6)]
    tail = jnp.concatenate([bias_sum[:, :half], bias_sum[:, half:]], axis=0)
    parts.append(jnp.broadcast_to(tail[None], (peers, 2, half)))
    send_ref[...] = jnp.concatenate(parts, axis=2).astype(BF16)


def feat_sum_kernel(got_ref, out_ref):
    total = jnp.sum(got_ref[...].astype(F32)[:, :, 512:], axis=0)
    out_ref[...] = jnp.broadcast_to(total.astype(BF16)[None], out_ref.shape)


def two_rows(value, at):
    return jnp.concatenate([value[:, at : at + 128], value[:, at + 128 : at + 256]], axis=0)


def rep_sum_kernel(factor, got_ref, after_ref, out_ref, bias_ref):
    total = factor * jnp.sum(got_ref[...].astype(F32), axis=0)
    bias_ref[...] = jnp.concatenate([total[0:1, 1024:], total[1:2, 1024:]], axis=1)
    whole = jnp.concatenate([two_rows(total, at) for at in (0, 256, 512, 768)], axis=1)
    out_ref[...] = jnp.broadcast_to(whole.astype(BF16)[None], out_ref.shape)


def assemble_kernel(
    got_ref, bias_ref, self_hbm, neigh_hbm, bias_hbm, self_ref, neigh_ref, sems
):
    side = got_ref.shape[2] // 4
    copies = [pltpu.make_async_copy(bias_ref, bias_hbm, sems.at[2])]
    copies[0].start()
    for j, (out_ref, out_hbm) in enumerate(((self_ref, self_hbm), (neigh_ref, neigh_hbm))):
        for h in range(2):
            at = (2 * h + j) * side
            got = got_ref[:, :, at : at + side].astype(F32)
            out_ref[:, h * side : (h + 1) * side] = got.reshape(-1, side)
        copy = pltpu.make_async_copy(out_ref, out_hbm, sems.at[j])
        copy.start()
        copies.append(copy)
    for copy in copies:
        copy.wait()


def backward_kernel(
    ids_ref, counts_ref, got_ref, hid_ref, held, adj_hbm, out_ref, hidden_ref, rest, acc, sems
):
    blocks, _, side, _ = adj_hbm.shape[1:]
    copy = pltpu.make_async_copy(
        adj_hbm.at[0, pl.ds(HELD, blocks - HELD)], rest, sems.at[0]
    )
    copy.start()
    hidden_ref[...] = hid_ref[...]
    acc[...] = jnp.zeros_like(acc)
    depth = ids_ref.shape[1]
    sources = acc.shape[0] - 1
    for b in range(blocks):
        if b == HELD:
            copy.wait()
        adj = held[b] if b < HELD else rest[b - HELD]
        count = counts_ref[0, b]
        lhs = two_rows(got_ref[FEAT_ORDER.index(b)].astype(F32), 2 * side).astype(BF16)
        contrib = lax.dot_general(
            lhs,
            adj.reshape(depth * side, side),
            (((1,), (1,)), ((), ())),
            preferred_element_type=F32,
        )
        for k in range(depth):
            place = jnp.where(k < count, ids_ref[0, k, b], sources)
            acc[place] = acc[place] + contrib[:, k * side : (k + 1) * side]
    for n in range(sources):
        total = acc[n]
        if n < blocks:
            total = total + two_rows(got_ref[FEAT_ORDER.index(n)].astype(F32), 0)
        out_ref[0, :, n * side : (n + 1) * side] = total.astype(BF16)


SMEM = pl.BlockSpec(memory_space=pltpu.SMEM)
VMEM = pl.BlockSpec(memory_space=pltpu.VMEM)
HBM = pl.BlockSpec(memory_space=pl.ANY)


def in_hbm(array):
    return pltpu.with_memory_space_constraint(array, pltpu.HBM)


def params(mib):
    return pltpu.CompilerParams(vmem_limit_bytes=mib * 1024 * 1024)


def local(
    feature_table,
    node_ids,
    block_ids,
    block_counts,
    adjacency,
    self_weight,
    neigh_weight,
    bias_vector,
    cotangent,
):
    chans = feature_table.shape[0]
    node_count = node_ids.shape[1]
    blocks, depth, side = adjacency.shape[1:4]
    sources = node_count // side
    peers = lax.axis_size("feat")
    reps = lax.axis_size("rep")
    feats, hid = self_weight.shape
    rows = cotangent.shape[1]
    lists = jnp.transpose(block_ids, (0, 2, 1))
    held_shape = (HELD, depth, side, side)
    rest_shape = (blocks - HELD, depth, side, side)
    sent, held = pl.pallas_call(
        forward_kernel,
        out_shape=(
            jax.ShapeDtypeStruct((peers, 8, side), BF16),
            jax.ShapeDtypeStruct(held_shape, BF16),
        ),
        in_specs=[HBM] * 5,
        out_specs=(VMEM, VMEM),
        scratch_shapes=[
            pltpu.VMEM(rest_shape, BF16),
            pltpu.SMEM(lists.shape, jnp.int32),
            pltpu.SMEM(block_counts.shape, jnp.int32),
            pltpu.VMEM(node_ids.shape, jnp.int32),
            pltpu.VMEM(feature_table.shape, BF16),
            pltpu.VMEM((feature_table.shape[1] // LOW * chans, LOW), F32),
            pltpu.VMEM((sources, 8, side), F32),
            pltpu.VMEM((peers, 8, side), F32),
            pltpu.SemaphoreType.DMA((6,)),
        ],
        compiler_params=params(24),
        name="forward",
    )(*[in_hbm(v) for v in (lists, block_counts, node_ids, feature_table, adjacency)])
    arrived = lax.all_to_all(
        sent, "feat", split_axis=0, concat_axis=0, tiled=True, axis_index_groups=[FEAT_ORDER]
    )
    hid_vmem, send = pl.pallas_call(
        dense_kernel,
        out_shape=(
            jax.ShapeDtypeStruct(cotangent.shape, BF16),
            jax.ShapeDtypeStruct((peers, 2, 13 * side), BF16),
        ),
        in_specs=[VMEM] * 5,
        out_specs=(VMEM, VMEM),
        compiler_params=params(16),
        name="dense",
    )(arrived, self_weight, neigh_weight, bias_vector.reshape(1, hid), cotangent)
    got = lax.all_to_all(
        send, "feat", split_axis=0, concat_axis=0, tiled=True, axis_index_groups=[FEAT_ORDER]
    )
    partial = pl.pallas_call(
        feat_sum_kernel,
        out_shape=jax.ShapeDtypeStruct((reps, 2, 9 * side), BF16),
        in_specs=[VMEM],
        out_specs=VMEM,
        compiler_params=params(8),
        name="feat_sum",
    )(got)
    order = [2 * ((3 * y) % (reps // 2)) + core for y in range(reps // 2) for core in range(2)]
    over_rep = lax.all_to_all(
        partial, "rep", split_axis=0, concat_axis=0, tiled=True, axis_index_groups=[order]
    )
    factor = float(rows * peers * reps) ** (-0.5)
    feature_grad, hidden = pl.pallas_call(
        backward_kernel,
        out_shape=(
            jax.ShapeDtypeStruct((1, chans, node_count), BF16),
            jax.ShapeDtypeStruct(cotangent.shape, BF16),
        ),
        in_specs=[SMEM, SMEM, VMEM, VMEM, VMEM, HBM],
        out_specs=(VMEM, VMEM),
        scratch_shapes=[
            pltpu.VMEM(rest_shape, BF16),
            pltpu.VMEM((sources + 1, chans, side), F32),
            pltpu.SemaphoreType.DMA((1,)),
        ],
        compiler_params=params(24),
        cost_estimate=pl.CostEstimate(
            flops=2 * 16 * adjacency.size, bytes_accessed=2 * adjacency.size, transcendentals=0
        ),
        name="spread_back",
    )(lists, block_counts, got, hid_vmem, held, in_hbm(adjacency))
    pieces, bias_sum = pl.pallas_call(
        lambda *refs: rep_sum_kernel(factor, *refs),
        out_shape=(
            jax.ShapeDtypeStruct((peers, chans, 4 * side), BF16),
            jax.ShapeDtypeStruct((1, hid), F32),
        ),
        in_specs=[VMEM, HBM],
        out_specs=(VMEM, VMEM),
        compiler_params=params(8),
        name="rep_sum",
    )(over_rep, in_hbm(hidden))
    whole = lax.all_to_all(pieces, "feat", split_axis=0, concat_axis=0, tiled=True)
    self_grad, neigh_grad, bias_grad = pl.pallas_call(
        assemble_kernel,
        out_shape=(
            jax.ShapeDtypeStruct((feats, hid), F32),
            jax.ShapeDtypeStruct((feats, hid), F32),
            jax.ShapeDtypeStruct((1, hid), F32),
        ),
        in_specs=[VMEM, VMEM],
        out_specs=(HBM, HBM, HBM),
        scratch_shapes=[
            pltpu.VMEM((feats, hid), F32),
            pltpu.VMEM((feats, hid), F32),
            pltpu.SemaphoreType.DMA((3,)),
        ],
        compiler_params=params(8),
        name="assemble",
    )(whole, bias_sum)
    return hidden, feature_grad, self_grad, neigh_grad, bias_grad.reshape(hid)


def solution(mesh):
    return jax.shard_map(
        local,
        mesh=mesh,
        in_specs=(
            P("feat", None),
            P("rep", None),
            P("rep", None, None),
            P("rep", None),
            P("rep", None, None, None, None),
            P(),
            P(),
            P(),
            P("rep", "feat", None),
        ),
        out_specs=(P("rep", "feat", None), P("rep", "feat", None), P(), P(), P()),
        check_vma=False,
    )
```
